32 devices in a mesh: row: 8 (over z, y), col: 4 (over x, core).
Axes of the slice: x: 2, y: 2, z: 4, core: 2. Of those that a mesh axis runs over, the one named last changes fastest.
Arguments:
- curl_tiles: bfloat16 [8, 128, 1024], P(None, 'col', 'row'), may hold values from -0.005859375 to 0.005859375
- gradient: bfloat16 [1024, 1536], P(('row', 'col')), may hold values from -6 to 6
- a_pattern: int32 [8, 8], replicated, may hold values 0 or 1
- g_pattern: int32 [8, 12], replicated, may hold values 0 or 1
Outputs:
- galerkin: float32 [1536, 1536], P('row', 'col')
The draws below stay inside these ranges and needn't reach their ends.
Inputs may be any that keep to these rules, and one draw needn't show every extreme that they name: `a_pattern`: 1 keeps a block in the pattern, 0 leaves it out. `g_pattern`: 1 keeps a block in the pattern, 0 leaves it out.
All inputs are finite; a program needn't handle non-finite values.
Results may differ from the reference program's by a relative error of at most 0.0003.
Values may be sent and summed in bfloat16 or wider, within the bound.
No kernel may reach another device: no remote copies, remote signals or barrier semaphores. Data moves between devices by JAX's collectives and lax.ppermute only.
A program may use at most 64 MiB of HBM per device.

```python
import jax
import jax.numpy as jnp
from jax import lax

BLOCK = 128
CB = 12
ROW_SPAN = 128
FINE = 1024
FINE_BLOCKS = 8
COARSE = 1536
N_ROW = 8


def with_ends(result, stream_key, low, high):
    dims = result.shape
    place = [jax.random.randint(jax.random.fold_in(stream_key, axis), (), 0, dims[axis]) for axis in range(len(dims))]
    result = result.at[tuple(place)].set(low)
    longest = dims.index(max(dims))
    place[longest] = (place[longest] + 1) % dims[longest]
    return result.at[tuple(place)].set(high)


def block_levels(key, shape, split, smallest, top_value):
    gain, own = 1.0, jax.random.fold_in(key, 6)
    for dim, shards_of in split:
        heights = jnp.exp(jax.random.uniform(jax.random.fold_in(own, dim), (shards_of,), jnp.float32, smallest / len(split), top_value / len(split)))
        gain = gain * jnp.repeat(heights, shape[dim] // shards_of).reshape([-1 if axis == dim else 1 for axis in range(len(shape))])
    return gain


def noise(own_key, extent, deviation, most, cuts=(), dtype=jnp.bfloat16):
    level = block_levels(own_key, extent, cuts, -0.22, 0.18) if cuts else 1.0
    values = jax.random.normal(own_key, extent, jnp.float32) * deviation * level
    return jnp.minimum(jnp.maximum(values, -most), most).astype(dtype)


def setup_inputs(seed: int = 0) -> dict:
    seeds = jax.random.split(jax.random.key(seed), 5)
    return {
        "curl_tiles": noise(seeds[0], (N_ROW, ROW_SPAN, FINE), (FINE * FINE) ** -0.5, 0.005859375, ((1, 4), (2, 8))),
        "gradient": noise(seeds[1], (FINE, COARSE), 1.0, 6.0, ((0, 32),)),
        "a_pattern": with_ends((jax.random.randint(seeds[2], (FINE_BLOCKS, FINE_BLOCKS), 0, 4) < 3).astype(jnp.int32), jax.random.fold_in(seeds[2], 1), 0, 1),
        "g_pattern": with_ends((jax.random.randint(seeds[3], (FINE_BLOCKS, CB), 0, 4) < 3).astype(jnp.int32), jax.random.fold_in(seeds[3], 1), 0, 1),
    }


def reference(curl_tiles, gradient, a_pattern, g_pattern):
    blocks = FINE // BLOCK
    a_full = jnp.transpose(curl_tiles.astype(jnp.float32), (2, 0, 1)).reshape(FINE, FINE)
    a_mask = a_pattern.astype(jnp.float32)[:, None, :, None]
    a_full = (a_full.reshape(blocks, BLOCK, blocks, BLOCK) * a_mask).reshape(FINE, FINE)
    g_mask = g_pattern.astype(jnp.float32)[:, None, :, None]
    g_full = (gradient.astype(jnp.float32).reshape(blocks, BLOCK, CB, BLOCK) * g_mask).reshape(FINE, COARSE)
    product = jnp.dot(a_full, g_full, precision=lax.Precision.HIGHEST, preferred_element_type=jnp.float32)
    return jnp.dot(g_full.T, product, precision=lax.Precision.HIGHEST, preferred_element_type=jnp.float32)
```

```python
import functools

import jax
import jax.numpy as jnp
from jax import lax
from jax.experimental import pallas as pl
from jax.experimental.pallas import tpu as pltpu
from jax.sharding import PartitionSpec as P

BLOCK = 128
GATHER_LIMIT = 8 * 1024 * 1024


def block_hits(position, block_total):
    return (position[:, None] // BLOCK == jnp.arange(block_total, dtype=jnp.int32)[None, :]).astype(
        jnp.float32
    )


def reducing_body(curl_tiles, gradient, a_pattern, g_pattern):
    row_count = lax.axis_size("row")
    row_pos = lax.axis_index("row")
    col_pos = lax.axis_index("col")
    rows_here = curl_tiles.shape[1]
    span_rows = curl_tiles.shape[2]
    fine_blocks = a_pattern.shape[0]
    strided_total = row_count * rows_here
    offsets = jnp.arange(rows_here, dtype=jnp.int32)
    column_index = (
        jnp.arange(row_count, dtype=jnp.int32)[:, None] * span_rows
        + col_pos * rows_here
        + offsets[None, :]
    ).reshape(-1)
    row_index = row_pos * span_rows + jnp.arange(span_rows, dtype=jnp.int32)
    own_index = row_pos * span_rows + col_pos * rows_here + offsets
    picked = jnp.dot(block_hits(row_index, fine_blocks), a_pattern.astype(jnp.float32))
    keep_a = jnp.dot(block_hits(column_index, fine_blocks), picked.T)
    masked_a = curl_tiles.reshape(strided_total, span_rows) * keep_a.astype(jnp.bfloat16)
    keep_g = jnp.dot(block_hits(own_index, fine_blocks), g_pattern.astype(jnp.float32))
    masked_g = gradient * jnp.repeat(keep_g, BLOCK, axis=1).astype(jnp.bfloat16)
    g_group = lax.all_gather(masked_g, "col", axis=0, tiled=True)
    g_strided = lax.all_gather(masked_g, "row", axis=0, tiled=True)
    product_t = lax.psum_scatter(
        lax.dot_general(
            g_strided, masked_a, (((0,), (0,)), ((), ())), preferred_element_type=jnp.float32
        ),
        "col",
        scatter_dimension=0,
        tiled=True,
    )
    return lax.psum_scatter(
        lax.dot_general(
            g_group.astype(jnp.float32),
            product_t,
            (((0,), (1,)), ((), ())),
            precision=lax.Precision.HIGHEST,
            preferred_element_type=jnp.float32,
        ),
        "row",
        scatter_dimension=0,
        tiled=True,
    )


def ring_row(position, count):
    return jnp.where(position < count // 2, 2 * position, 2 * (count - 1 - position) + 1)


def ring_position(row, count):
    return jnp.where(row % 2 == 0, row // 2, count - 1 - row // 2)


def ring_rows(count):
    return list(range(0, count, 2)) + list(range(count - 1, 0, -2))


def pack_kernel(a_pattern, g_pattern, a_ref, g_ref, out_ref):
    row = lax.axis_index("row")
    tiles, rows_here, _ = a_ref.shape
    for k in range(tiles):
        out_ref[k * rows_here : (k + 1) * rows_here, :] = jnp.where(a_pattern[row, k] != 0, a_ref[k], 0)
    base = tiles * rows_here
    for j in range(g_ref.shape[1] // BLOCK):
        out_ref[base + j * rows_here : base + (j + 1) * rows_here, :] = jnp.where(
            g_pattern[row, j] != 0, g_ref[:, j * BLOCK : (j + 1) * BLOCK], 0
        )


def product_kernel(count, rows_here, *refs):
    pieces = [refs[4 * d : 4 * d + 4] for d in range(count)]
    out_ref, g_cols, g_rows, total = refs[4 * count :]
    row, col = lax.axis_index("row"), lax.axis_index("col")
    position = ring_position(row, count)
    a_rows = count * rows_here
    out_rows, out_cols = out_ref.shape
    col_blocks, row_blocks = out_cols // BLOCK, g_rows.shape[1] // BLOCK
    first_col = col * col_blocks
    first_row = (row * out_rows) // BLOCK
    for d in range(count):
        source = ring_row(lax.rem(position - d + count, count), count)
        for m in range(4):
            ref = pieces[d][m]
            below = pl.ds(pl.multiple_of(m * a_rows + source * rows_here, 32), rows_here)
            for j in range(col_blocks):
                start = pl.multiple_of(a_rows + (first_col + j) * rows_here, 32)
                g_cols[below, j * BLOCK : (j + 1) * BLOCK] = ref[pl.ds(start, rows_here), :]
            below = pl.ds(pl.multiple_of(d * BLOCK + (col ^ m) * rows_here, 32), rows_here)
            for j in range(row_blocks):
                start = pl.multiple_of(a_rows + (first_row + j) * rows_here, 32)
                g_rows[below, j * BLOCK : (j + 1) * BLOCK] = ref[pl.ds(start, rows_here), :]
    for m in range(4):
        part = None
        for d in range(0, count, 2):
            a = jnp.concatenate([pieces[d][m][:a_rows, :], pieces[d + 1][m][:a_rows, :]], axis=1)
            term = lax.dot_general(
                g_rows[d * BLOCK : (d + 2) * BLOCK, :],
                a,
                (((0,), (1,)), ((), ())),
                preferred_element_type=jnp.float32,
            )
            part = term if part is None else part + term
        high = part.astype(jnp.bfloat16)
        rest = part - high.astype(jnp.float32)
        middle = rest.astype(jnp.bfloat16)
        low = (rest - middle.astype(jnp.float32)).astype(jnp.bfloat16)
        g = g_cols[m * a_rows : (m + 1) * a_rows, :]
        term = sum(jnp.dot(x, g, preferred_element_type=jnp.float32) for x in (low, middle, high))
        if m == 0:
            total[...] = term
        else:
            total[...] += term
    shift = pl.multiple_of(row * out_rows - first_row * BLOCK, 64)
    out_ref[...] = total[pl.ds(shift, out_rows), :]


def gathering_body(count, curl_tiles, gradient, a_pattern, g_pattern):
    rows_here = curl_tiles.shape[1]
    coarse = gradient.shape[1]
    out_rows, out_cols = coarse // count, coarse // 4
    a_rows = count * rows_here
    own = pl.pallas_call(
        pack_kernel,
        out_shape=jax.ShapeDtypeStruct((a_rows + coarse // BLOCK * rows_here, BLOCK), jnp.bfloat16),
        in_specs=[pl.BlockSpec(memory_space=pltpu.SMEM)] * 2 + [pl.BlockSpec(memory_space=pltpu.VMEM)] * 2,
        out_specs=pl.BlockSpec(memory_space=pltpu.VMEM),
        name="pack",
    )(a_pattern, g_pattern, curl_tiles, gradient)
    order = ring_rows(count)
    axes = ("row", "col")

    def along(step):
        return [
            (order[p] * 4 + c, order[(p + step) % count] * 4 + c) for p in range(count) for c in range(4)
        ]

    def across(mask):
        return [(i, i ^ mask) for i in range(4 * count)]

    forward, backward = along(1), along(-1)
    held = {(0, 0): own, (0, 2): lax.ppermute(own, axes, across(2))}
    half = count // 2
    for step in range(1, half):
        for m in (0, 2):
            held[step, m] = lax.ppermute(held[step - 1, m], axes, forward)
            held[count - step, m] = lax.ppermute(held[(count - step + 1) % count, m], axes, backward)
    held[half, 0] = lax.ppermute(held[half - 1, 0], axes, forward)
    held[half, 2] = lax.ppermute(held[half + 1, 2], axes, backward)
    for (d, m), piece in list(held.items()):
        held[d, m + 1] = lax.ppermute(piece, axes, across(1))
    window = -(-(out_rows + 64) // BLOCK) * BLOCK
    return pl.pallas_call(
        functools.partial(product_kernel, count, rows_here),
        out_shape=jax.ShapeDtypeStruct((out_rows, out_cols), jnp.float32),
        in_specs=[pl.BlockSpec(memory_space=pltpu.VMEM)] * (4 * count),
        out_specs=pl.BlockSpec(memory_space=pltpu.VMEM),
        scratch_shapes=[
            pltpu.VMEM((4 * a_rows, out_cols), jnp.bfloat16),
            pltpu.VMEM((4 * a_rows, window), jnp.bfloat16),
            pltpu.VMEM((window, out_cols), jnp.float32),
        ],
        compiler_params=pltpu.CompilerParams(vmem_limit_bytes=16 * 1024 * 1024),
        name="product",
    )(*(held[d, m] for d in range(count) for m in range(4)))


def gathers(mesh, curl_tiles, gradient):
    count, width = mesh.shape["row"], mesh.shape["col"]
    coarse = gradient.shape[1]
    return (
        width == 4
        and count % 2 == 0
        and curl_tiles.shape[2] // count == BLOCK
        and curl_tiles.shape[1] // width == 32
        and coarse % (width * BLOCK) == 0
        and coarse % (count * 64) == 0
        and 2 * (curl_tiles.size + gradient.size) <= GATHER_LIMIT
    )


def solution(mesh):
    placed = (P(None, "col", "row"), P(("row", "col"), None), P(), P())

    def run(curl_tiles, gradient, a_pattern, g_pattern):
        body = reducing_body
        if gathers(mesh, curl_tiles, gradient):
            body = functools.partial(gathering_body, mesh.shape["row"])
        return jax.shard_map(
            body, mesh=mesh, in_specs=placed, out_specs=P("row", "col"), check_vma=False
        )(curl_tiles, gradient, a_pattern, g_pattern)

    return run
```

```python
import functools

import jax
import jax.numpy as jnp
from jax import lax
from jax.experimental import pallas as pl
from jax.experimental.pallas import tpu as pltpu
from jax.sharding import PartitionSpec as P

BLOCK = 128
GATHER_LIMIT = 8 * 1024 * 1024


def block_hits(position, block_total):
    return (position[:, None] // BLOCK == jnp.arange(block_total, dtype=jnp.int32)[None, :]).astype(
        jnp.float32
    )


def reducing_body(curl_tiles, gradient, a_pattern, g_pattern):
    row_count = lax.axis_size("row")
    row_pos = lax.axis_index("row")
    col_pos = lax.axis_index("col")
    rows_here = curl_tiles.shape[1]
    span_rows = curl_tiles.shape[2]
    fine_blocks = a_pattern.shape[0]
    strided_total = row_count * rows_here
    offsets = jnp.arange(rows_here, dtype=jnp.int32)
    column_index = (
        jnp.arange(row_count, dtype=jnp.int32)[:, None] * span_rows
        + col_pos * rows_here
        + offsets[None, :]
    ).reshape(-1)
    row_index = row_pos * span_rows + jnp.arange(span_rows, dtype=jnp.int32)
    own_index = row_pos * span_rows + col_pos * rows_here + offsets
    picked = jnp.dot(block_hits(row_index, fine_blocks), a_pattern.astype(jnp.float32))
    keep_a = jnp.dot(block_hits(column_index, fine_blocks), picked.T)
    masked_a = curl_tiles.reshape(strided_total, span_rows) * keep_a.astype(jnp.bfloat16)
    keep_g = jnp.dot(block_hits(own_index, fine_blocks), g_pattern.astype(jnp.float32))
    masked_g = gradient * jnp.repeat(keep_g, BLOCK, axis=1).astype(jnp.bfloat16)
    g_group = lax.all_gather(masked_g, "col", axis=0, tiled=True)
    g_strided = lax.all_gather(masked_g, "row", axis=0, tiled=True)
    product_t = lax.psum_scatter(
        lax.dot_general(
            g_strided, masked_a, (((0,), (0,)), ((), ())), preferred_element_type=jnp.float32
        ),
        "col",
        scatter_dimension=0,
        tiled=True,
    )
    return lax.psum_scatter(
        lax.dot_general(
            g_group.astype(jnp.float32),
            product_t,
            (((0,), (1,)), ((), ())),
            precision=lax.Precision.HIGHEST,
            preferred_element_type=jnp.float32,
        ),
        "row",
        scatter_dimension=0,
        tiled=True,
    )


def ring_row(position, count):
    return jnp.where(position < count // 2, 2 * position, 2 * (count - 1 - position) + 1)


def ring_position(row, count):
    return jnp.where(row % 2 == 0, row // 2, count - 1 - row // 2)


def ring_rows(count):
    return list(range(0, count, 2)) + list(range(count - 1, 0, -2))


def layout(count, rows_here, coarse):
    a_rows = count * rows_here
    col_blocks = coarse // 4 // BLOCK
    row_blocks = -(-(coarse // count + 64) // BLOCK)
    crossing = a_rows + (2 * col_blocks + row_blocks) * rows_here
    share = a_rows + (col_blocks + row_blocks) * rows_here
    return a_rows, col_blocks, row_blocks, crossing, share


def first_window(row, count, coarse):
    return (row * (coarse // count)) // BLOCK


def aligned(start):
    return pl.multiple_of(start, 32)


def put(out_ref, at, ref, start, rows):
    out_ref[at : at + rows, :] = ref[pl.ds(start, rows), :]
    return at + rows


def cut_kernel(count, rows_here, coarse, items, *refs):
    a_rows, col_blocks, row_blocks, _, _ = layout(count, rows_here, coarse)
    row, col = lax.axis_index("row"), lax.axis_index("col")
    second = col % 2 == 1
    for (sources, steps, over), out_ref in zip(items, refs[len(refs) - len(items) :]):
        step = jnp.where(second, steps[1] + count, steps[0] + count)
        there = ring_row(lax.rem(ring_position(row, count) + step, count), count)
        half = aligned(a_rows + ((col // 2) ^ over) * (2 * col_blocks * rows_here))
        window = aligned(a_rows + first_window(there, count, coarse) * rows_here)
        at = 0
        for start, n in ((0, a_rows), (half, 2 * col_blocks * rows_here), (window, row_blocks * rows_here)):
            part = refs[sources[0]][pl.ds(start, n), :]
            if sources[1] != sources[0]:
                part = jnp.where(second, refs[sources[1]][pl.ds(start, n), :], part)
            out_ref[at : at + n, :] = part
            at += n


def pack_kernel(count, rows_here, coarse, a_pattern, g_pattern, a_ref, g_ref, out_ref):
    row = lax.axis_index("row")
    a_rows = layout(count, rows_here, coarse)[0]
    for k in range(count):
        out_ref[k * rows_here : (k + 1) * rows_here, :] = jnp.where(a_pattern[row, k] != 0, a_ref[k], 0)
    for j in range(coarse // BLOCK):
        out_ref[a_rows + j * rows_here : a_rows + (j + 1) * rows_here, :] = jnp.where(
            g_pattern[row, j] != 0, g_ref[:, j * BLOCK : (j + 1) * BLOCK], 0
        )


class Piece:
    def __init__(self, kind, ref, begin, sizes):
        self.kind, self.ref, self.begin, self.sizes = kind, ref, begin, sizes

    def tiles(self):
        return self.ref[self.begin : self.begin + self.sizes[0], :]

    def columns(self, rows_here, col):
        a_rows, col_blocks = self.sizes[:2]
        start = self.begin + a_rows
        if self.kind == "whole":
            start = aligned(start + col * (col_blocks * rows_here))
        elif self.kind == "cross":
            start = aligned(start + (col % 2) * (col_blocks * rows_here))
        return start

    def window(self, rows_here, first):
        a_rows, col_blocks = self.sizes[:2]
        start = self.begin + a_rows
        if self.kind == "whole":
            return aligned(start + first * rows_here)
        return start + (2 if self.kind == "cross" else 1) * col_blocks * rows_here


def pieces_of(spec, refs, sizes):
    return {key: Piece(kind, refs[index], begin, sizes) for key, (kind, index, begin) in spec.items()}


def collect_kernel(count, rows_here, coarse, spec, *refs):
    sizes = layout(count, rows_here, coarse)
    a_rows, col_blocks, row_blocks = sizes[:3]
    row, col = lax.axis_index("row"), lax.axis_index("col")
    first = first_window(row, count, coarse)
    for out_ref, owner in ((refs[-2], col), (refs[-1], col ^ 1)):
        at = 0
        for piece in pieces_of(spec, refs, sizes).values():
            at = put(out_ref, at, piece.ref, piece.begin, a_rows)
            at = put(out_ref, at, piece.ref, piece.columns(rows_here, owner), col_blocks * rows_here)
            at = put(out_ref, at, piece.ref, piece.window(rows_here, first), row_blocks * rows_here)


def place_kernel_part(pieces, count, rows_here, coarse, distances, g_cols, g_rows):
    _, col_blocks, row_blocks, _, _ = layout(count, rows_here, coarse)
    a_rows = count * rows_here
    row, col = lax.axis_index("row"), lax.axis_index("col")
    position = ring_position(row, count)
    first = first_window(row, count, coarse)
    for (d, m), piece in pieces.items():
        source = ring_row(lax.rem(position - d + count, count), count)
        if g_cols is not None:
            below = pl.ds(aligned(m * a_rows + source * rows_here), rows_here)
            start = piece.columns(rows_here, col)
            for j in range(col_blocks):
                g_cols[below, j * BLOCK : (j + 1) * BLOCK] = piece.ref[pl.ds(start + j * rows_here, rows_here), :]
        if d in distances:
            below = pl.ds(aligned(distances.index(d) * BLOCK + (col ^ m) * rows_here), rows_here)
            start = piece.window(rows_here, first)
            for j in range(row_blocks):
                g_rows[below, j * BLOCK : (j + 1) * BLOCK] = piece.ref[pl.ds(start + j * rows_here, rows_here), :]


def partial_product(pieces, m, distances, g_rows):
    part = None
    for i in range(0, len(distances), 2):
        pair = distances[i : i + 2]
        tiles = [pieces[d, m].tiles() for d in pair]
        term = lax.dot_general(
            g_rows[i * BLOCK : (i + len(pair)) * BLOCK, :],
            tiles[0] if len(tiles) == 1 else jnp.concatenate(tiles, axis=1),
            (((0,), (1,)), ((), ())),
            preferred_element_type=jnp.float32,
        )
        part = term if part is None else part + term
    return part


def early_kernel(count, rows_here, coarse, spec, distances, *refs):
    part_ref, g_cols, g_rows = refs[-3:]
    sizes = layout(count, rows_here, coarse)
    a_rows = sizes[0]
    pieces = pieces_of(spec, refs, sizes)
    place_kernel_part(pieces, count, rows_here, coarse, distances, g_cols, g_rows)
    for m in range(4):
        part_ref[:, m * a_rows : (m + 1) * a_rows] = partial_product(pieces, m, distances, g_rows)


def product_kernel(count, rows_here, coarse, late, spec, distances, *refs):
    part_ref, g_early, out_ref, g_cols, g_rows, total, highs, lows = refs[-8:]
    sizes = layout(count, rows_here, coarse)
    a_rows = sizes[0]
    pieces = pieces_of(spec, refs, sizes)
    g_cols[...] = g_early[...]
    place_kernel_part({key: pieces[key] for key in late}, count, rows_here, coarse, distances, g_cols, g_rows)
    rest = {key: piece for key, piece in pieces.items() if key not in late}
    place_kernel_part(rest, count, rows_here, coarse, distances, None, g_rows)
    for m in range(4):
        columns = slice(m * a_rows, (m + 1) * a_rows)
        part = part_ref[:, columns] + partial_product(pieces, m, distances, g_rows)
        high = part.astype(jnp.bfloat16)
        highs[:, columns] = high
        lows[:, columns] = (part - high.astype(jnp.float32)).astype(jnp.bfloat16)
    total[...] = jnp.dot(lows[...], g_cols[...], preferred_element_type=jnp.float32) + jnp.dot(
        highs[...], g_cols[...], preferred_element_type=jnp.float32
    )
    row = lax.axis_index("row")
    out_rows = out_ref.shape[0]
    shift = pl.multiple_of(row * out_rows - first_window(row, count, coarse) * BLOCK, 64)
    out_ref[...] = total[pl.ds(shift, out_rows), :]


def gathering_body(count, curl_tiles, gradient, a_pattern, g_pattern):
    rows_here = curl_tiles.shape[1]
    coarse = gradient.shape[1]
    out_rows, out_cols = coarse // count, coarse // 4
    a_rows, _, row_blocks, crossing, share = layout(count, rows_here, coarse)
    packed = a_rows + coarse // BLOCK * rows_here
    whole, scalars = pl.BlockSpec(memory_space=pltpu.VMEM), pl.BlockSpec(memory_space=pltpu.SMEM)
    limit = pltpu.CompilerParams(vmem_limit_bytes=8 * 1024 * 1024)
    sizes = (count, rows_here, coarse)
    axes = ("row", "col")

    def rows(n):
        return pltpu.VMEM((n, BLOCK), jnp.bfloat16)

    def call(kernel, out, operands, name, *given, **options):
        return pl.pallas_call(
            functools.partial(kernel, *sizes, *given),
            out_shape=out,
            in_specs=options.pop("in_specs", [whole] * len(operands)),
            out_specs=[whole] * len(out) if isinstance(out, list) else whole,
            name=name,
            **options,
        )(*operands)

    order = ring_rows(count)

    def along(step):
        return [
            (order[p] * 4 + c, order[(p + step) % count] * 4 + c) for p in range(count) for c in range(4)
        ]

    def across(piece, mask):
        return lax.ppermute(piece, axes, [(i, i ^ mask) for i in range(4 * count)])

    forward, backward = along(1), along(-1)
    half = count // 2
    own = call(
        pack_kernel,
        rows(packed),
        (a_pattern, g_pattern, curl_tiles, gradient),
        "pack",
        in_specs=[scalars] * 2 + [whole] * 2,
    )
    held = {(0, 0): ("whole", own, 0), (0, 2): ("whole", across(own, 2), 0)}

    def operands_of(pieces):
        buffers, spec = [], {}
        for key, (kind, buffer, begin) in pieces.items():
            if not any(buffer is b for b in buffers):
                buffers.append(buffer)
            spec[key] = (kind, [buffer is b for b in buffers].index(True), begin)
        return buffers, spec

    def exchange(pieces, *over):
        buffers, spec = operands_of(pieces)
        mine, theirs = call(
            collect_kernel,
            [rows(len(pieces) * share)] * 2,
            [*buffers, *over],
            "collect",
            spec,
            compiler_params=limit,
        )
        theirs = across(theirs, 1)
        return {
            (d, m + other): ("share", (mine, theirs)[other], i * share)
            for i, (d, m) in enumerate(spec)
            for other in (0, 1)
        }

    def cut(items, *operands):
        return call(cut_kernel, [rows(crossing)] * len(items), operands, "cut", items, compiler_params=limit)

    for m in (0, 2):
        ahead = back = held[0, m][1]
        for step in range(1, half):
            if m == 2 and step == half - 1:
                ahead, back = cut([((0, 0), (1, 1), 0), ((1, 1), (-1, -1), 0)], ahead, back)
            ahead, back = lax.ppermute(ahead, axes, forward), lax.ppermute(back, axes, backward)
            kind = "cross" if m == 2 and step == half - 1 else "whole"
            held[step, m], held[count - step, m] = (kind, ahead, 0), (kind, back, 0)
    split = [pair for pair in forward if pair[0] % 2 == 0] + [pair for pair in backward if pair[0] % 2 == 1]
    straight, diagonal = cut(
        [((0, 1), (1, -1), 0), ((0, 1), (1, -1), 1)], held[half - 1, 0][1], held[half + 1, 0][1]
    )
    held[half, 0] = ("cross", lax.ppermute(straight, axes, split), 0)
    held[half, 2] = ("cross", lax.ppermute(diagonal, axes, [(i, j ^ 2) for i, j in split]), 0)
    early = {key: held[key] for key in held if min(key[0], count - key[0]) <= (3, 2)[key[1] // 2]}
    got = exchange(early)
    distances = [d for d in range(count) if (d, 0) in early and (d, 2) in early]
    buffers, spec = operands_of(got)
    part, g_cols = call(
        early_kernel,
        [
            pltpu.VMEM((row_blocks * BLOCK, 4 * a_rows), jnp.float32),
            pltpu.VMEM((4 * a_rows, out_cols), jnp.bfloat16),
        ],
        buffers,
        "early",
        spec,
        distances,
        scratch_shapes=[pltpu.VMEM((len(distances) * BLOCK, row_blocks * BLOCK), jnp.bfloat16)],
        compiler_params=limit,
    )
    late = {key: piece for key, piece in held.items() if key not in early}
    late.update({(d, m + 1): (kind, across(piece, 1), begin) for (d, m), (kind, piece, begin) in list(late.items())})
    late_distances = [d for d in range(count) if d not in distances]
    last_pieces = {**late, **{key: p for key, p in got.items() if key[0] in late_distances}}
    buffers, spec = operands_of(last_pieces)
    return call(
        product_kernel,
        jax.ShapeDtypeStruct((out_rows, out_cols), jnp.float32),
        buffers + [part, g_cols],
        "product",
        tuple(late),
        spec,
        late_distances,
        scratch_shapes=[
            pltpu.VMEM((4 * a_rows, out_cols), jnp.bfloat16),
            pltpu.VMEM((len(late_distances) * BLOCK, row_blocks * BLOCK), jnp.bfloat16),
            pltpu.VMEM((row_blocks * BLOCK, out_cols), jnp.float32),
            *[pltpu.VMEM((row_blocks * BLOCK, 4 * a_rows), jnp.bfloat16)] * 2,
        ],
        compiler_params=limit,
    )


def gathers(mesh, curl_tiles, gradient):
    count, width = mesh.shape["row"], mesh.shape["col"]
    coarse = gradient.shape[1]
    return (
        width == 4
        and count % 2 == 0
        and curl_tiles.shape[2] // count == BLOCK
        and curl_tiles.shape[1] // width == 32
        and coarse % (width * BLOCK) == 0
        and coarse % (count * 64) == 0
        and 2 * (curl_tiles.size + gradient.size) <= GATHER_LIMIT
    )


def solution(mesh):
    placed = (P(None, "col", "row"), P(("row", "col"), None), P(), P())

    def run(curl_tiles, gradient, a_pattern, g_pattern):
        body = reducing_body
        if gathers(mesh, curl_tiles, gradient):
            body = functools.partial(gathering_body, mesh.shape["row"])
        return jax.shard_map(
            body, mesh=mesh, in_specs=placed, out_specs=P("row", "col"), check_vma=False
        )(curl_tiles, gradient, a_pattern, g_pattern)

    return run
```

```python
import functools

import jax
import jax.numpy as jnp
from jax import lax
from jax.experimental import pallas as pl
from jax.experimental.pallas import tpu as pltpu
from jax.sharding import PartitionSpec as P

BLOCK = 128
GATHER_LIMIT = 8 * 1024 * 1024


def block_hits(position, block_total):
    return (position[:, None] // BLOCK == jnp.arange(block_total, dtype=jnp.int32)[None, :]).astype(
        jnp.float32
    )


def reducing_body(curl_tiles, gradient, a_pattern, g_pattern):
    row_count = lax.axis_size("row")
    row_pos = lax.axis_index("row")
    col_pos = lax.axis_index("col")
    rows_here = curl_tiles.shape[1]
    span_rows = curl_tiles.shape[2]
    fine_blocks = a_pattern.shape[0]
    strided_total = row_count * rows_here
    offsets = jnp.arange(rows_here, dtype=jnp.int32)
    column_index = (
        jnp.arange(row_count, dtype=jnp.int32)[:, None] * span_rows
        + col_pos * rows_here
        + offsets[None, :]
    ).reshape(-1)
    row_index = row_pos * span_rows + jnp.arange(span_rows, dtype=jnp.int32)
    own_index = row_pos * span_rows + col_pos * rows_here + offsets
    picked = jnp.dot(block_hits(row_index, fine_blocks), a_pattern.astype(jnp.float32))
    keep_a = jnp.dot(block_hits(column_index, fine_blocks), picked.T)
    masked_a = curl_tiles.reshape(strided_total, span_rows) * keep_a.astype(jnp.bfloat16)
    keep_g = jnp.dot(block_hits(own_index, fine_blocks), g_pattern.astype(jnp.float32))
    masked_g = gradient * jnp.repeat(keep_g, BLOCK, axis=1).astype(jnp.bfloat16)
    g_group = lax.all_gather(masked_g, "col", axis=0, tiled=True)
    g_strided = lax.all_gather(masked_g, "row", axis=0, tiled=True)
    product_t = lax.psum_scatter(
        lax.dot_general(
            g_strided, masked_a, (((0,), (0,)), ((), ())), preferred_element_type=jnp.float32
        ),
        "col",
        scatter_dimension=0,
        tiled=True,
    )
    return lax.psum_scatter(
        lax.dot_general(
            g_group.astype(jnp.float32),
            product_t,
            (((0,), (1,)), ((), ())),
            precision=lax.Precision.HIGHEST,
            preferred_element_type=jnp.float32,
        ),
        "row",
        scatter_dimension=0,
        tiled=True,
    )


def ring_row(position, count):
    return jnp.where(position < count // 2, 2 * position, 2 * (count - 1 - position) + 1)


def ring_position(row, count):
    return jnp.where(row % 2 == 0, row // 2, count - 1 - row // 2)


def ring_rows(count):
    return list(range(0, count, 2)) + list(range(count - 1, 0, -2))


def layout(count, rows_here, coarse):
    a_rows = count * rows_here
    col_blocks = coarse // 4 // BLOCK
    row_blocks = -(-(coarse // count + 64) // BLOCK)
    crossing = a_rows + (2 * col_blocks + row_blocks) * rows_here
    share = a_rows + (col_blocks + row_blocks) * rows_here
    return a_rows, col_blocks, row_blocks, crossing, share


def first_window(row, count, coarse):
    return (row * (coarse // count)) // BLOCK


def aligned(start):
    return pl.multiple_of(start, 32)


def put(out_ref, at, ref, start, rows):
    out_ref[at : at + rows, :] = ref[pl.ds(start, rows), :]
    return at + rows


def cut_kernel(count, rows_here, coarse, items, *refs):
    a_rows, col_blocks, row_blocks, _, _ = layout(count, rows_here, coarse)
    row, col = lax.axis_index("row"), lax.axis_index("col")
    second = col % 2 == 1
    for (sources, steps, over), out_ref in zip(items, refs[len(refs) - len(items) :]):
        step = jnp.where(second, steps[1] + count, steps[0] + count)
        there = ring_row(lax.rem(ring_position(row, count) + step, count), count)
        half = aligned(a_rows + ((col // 2) ^ over) * (2 * col_blocks * rows_here))
        window = aligned(a_rows + first_window(there, count, coarse) * rows_here)
        at = 0
        for start, n in ((0, a_rows), (half, 2 * col_blocks * rows_here), (window, row_blocks * rows_here)):
            part = refs[sources[0]][pl.ds(start, n), :]
            if sources[1] != sources[0]:
                part = jnp.where(second, refs[sources[1]][pl.ds(start, n), :], part)
            out_ref[at : at + n, :] = part
            at += n


def pack_kernel(count, rows_here, coarse, a_pattern, g_pattern, a_ref, g_ref, out_ref):
    row = lax.axis_index("row")
    a_rows = layout(count, rows_here, coarse)[0]
    for k in range(count):
        out_ref[k * rows_here : (k + 1) * rows_here, :] = jnp.where(a_pattern[row, k] != 0, a_ref[k], 0)
    for j in range(coarse // BLOCK):
        out_ref[a_rows + j * rows_here : a_rows + (j + 1) * rows_here, :] = jnp.where(
            g_pattern[row, j] != 0, g_ref[:, j * BLOCK : (j + 1) * BLOCK], 0
        )


class Piece:
    def __init__(self, kind, ref, begin, sizes):
        self.kind, self.ref, self.begin, self.sizes = kind, ref, begin, sizes

    def tiles(self):
        return self.ref[self.begin : self.begin + self.sizes[0], :]

    def columns(self, rows_here, col):
        a_rows, col_blocks = self.sizes[:2]
        start = self.begin + a_rows
        if self.kind == "whole":
            start = aligned(start + col * (col_blocks * rows_here))
        elif self.kind == "cross":
            start = aligned(start + (col % 2) * (col_blocks * rows_here))
        return start

    def window(self, rows_here, first):
        a_rows, col_blocks = self.sizes[:2]
        start = self.begin + a_rows
        if self.kind == "whole":
            return aligned(start + first * rows_here)
        return start + (2 if self.kind == "cross" else 1) * col_blocks * rows_here


def pieces_of(spec, refs, sizes):
    return {key: Piece(kind, refs[index], begin, sizes) for key, (kind, index, begin) in spec.items()}


def collect_kernel(count, rows_here, coarse, spec, *refs):
    sizes = layout(count, rows_here, coarse)
    a_rows, col_blocks, row_blocks = sizes[:3]
    row, col = lax.axis_index("row"), lax.axis_index("col")
    first = first_window(row, count, coarse)
    for out_ref, owner in ((refs[-2], col), (refs[-1], col ^ 1)):
        at = 0
        for piece in pieces_of(spec, refs, sizes).values():
            at = put(out_ref, at, piece.ref, piece.begin, a_rows)
            at = put(out_ref, at, piece.ref, piece.columns(rows_here, owner), col_blocks * rows_here)
            at = put(out_ref, at, piece.ref, piece.window(rows_here, first), row_blocks * rows_here)


def place_kernel_part(pieces, count, rows_here, coarse, distances, g_cols, g_rows):
    _, col_blocks, row_blocks, _, _ = layout(count, rows_here, coarse)
    a_rows = count * rows_here
    row, col = lax.axis_index("row"), lax.axis_index("col")
    position = ring_position(row, count)
    first = first_window(row, count, coarse)
    for (d, m), piece in pieces.items():
        source = ring_row(lax.rem(position - d + count, count), count)
        if g_cols is not None:
            below = pl.ds(aligned(m * a_rows + source * rows_here), rows_here)
            start = piece.columns(rows_here, col)
            for j in range(col_blocks):
                g_cols[below, j * BLOCK : (j + 1) * BLOCK] = piece.ref[pl.ds(start + j * rows_here, rows_here), :]
        if d in distances:
            below = pl.ds(aligned(distances.index(d) * BLOCK + (col ^ m) * rows_here), rows_here)
            start = piece.window(rows_here, first)
            for j in range(row_blocks):
                g_rows[below, j * BLOCK : (j + 1) * BLOCK] = piece.ref[pl.ds(start + j * rows_here, rows_here), :]


def partial_product(pieces, m, distances, g_rows):
    part = None
    for i in range(0, len(distances), 2):
        pair = distances[i : i + 2]
        tiles = [pieces[d, m].tiles() for d in pair]
        term = lax.dot_general(
            g_rows[i * BLOCK : (i + len(pair)) * BLOCK, :],
            tiles[0] if len(tiles) == 1 else jnp.concatenate(tiles, axis=1),
            (((0,), (1,)), ((), ())),
            preferred_element_type=jnp.float32,
        )
        part = term if part is None else part + term
    return part


def early_kernel(count, rows_here, coarse, spec, distances, *refs):
    part_ref, g_cols, g_rows = refs[-3:]
    sizes = layout(count, rows_here, coarse)
    a_rows = sizes[0]
    pieces = pieces_of(spec, refs, sizes)
    place_kernel_part(pieces, count, rows_here, coarse, distances, g_cols, g_rows)
    for m in range(4):
        part_ref[:, m * a_rows : (m + 1) * a_rows] = partial_product(pieces, m, distances, g_rows)


def product_kernel(count, rows_here, coarse, late, spec, distances, *refs):
    part_ref, g_early, out_ref, g_cols, g_rows, total, highs, lows = refs[-8:]
    sizes = layout(count, rows_here, coarse)
    a_rows = sizes[0]
    pieces = pieces_of(spec, refs, sizes)
    g_cols[...] = g_early[...]
    place_kernel_part({key: pieces[key] for key in late}, count, rows_here, coarse, distances, g_cols, g_rows)
    rest = {key: piece for key, piece in pieces.items() if key not in late}
    place_kernel_part(rest, count, rows_here, coarse, distances, None, g_rows)
    for m in range(4):
        columns = slice(m * a_rows, (m + 1) * a_rows)
        part = part_ref[:, columns] + partial_product(pieces, m, distances, g_rows)
        high = part.astype(jnp.bfloat16)
        highs[:, columns] = high
        lows[:, columns] = (part - high.astype(jnp.float32)).astype(jnp.bfloat16)
    total[...] = jnp.dot(lows[...], g_cols[...], preferred_element_type=jnp.float32) + jnp.dot(
        highs[...], g_cols[...], preferred_element_type=jnp.float32
    )
    row = lax.axis_index("row")
    out_rows = out_ref.shape[0]
    shift = pl.multiple_of(row * out_rows - first_window(row, count, coarse) * BLOCK, 64)
    out_ref[...] = total[pl.ds(shift, out_rows), :]


def gathering_body(count, curl_tiles, gradient, a_pattern, g_pattern):
    rows_here = curl_tiles.shape[1]
    coarse = gradient.shape[1]
    out_rows, out_cols = coarse // count, coarse // 4
    a_rows, _, row_blocks, crossing, share = layout(count, rows_here, coarse)
    packed = a_rows + coarse // BLOCK * rows_here
    whole, scalars = pl.BlockSpec(memory_space=pltpu.VMEM), pl.BlockSpec(memory_space=pltpu.SMEM)
    limit = pltpu.CompilerParams(vmem_limit_bytes=8 * 1024 * 1024)
    sizes = (count, rows_here, coarse)
    axes = ("row", "col")

    def rows(n):
        return pltpu.VMEM((n, BLOCK), jnp.bfloat16)

    def call(kernel, out, operands, name, *given, **options):
        return pl.pallas_call(
            functools.partial(kernel, *sizes, *given),
            out_shape=out,
            in_specs=options.pop("in_specs", [whole] * len(operands)),
            out_specs=[whole] * len(out) if isinstance(out, list) else whole,
            name=name,
            **options,
        )(*operands)

    order = ring_rows(count)

    def along(step):
        return [
            (order[p] * 4 + c, order[(p + step) % count] * 4 + c) for p in range(count) for c in range(4)
        ]

    def across(piece, mask):
        return lax.ppermute(piece, axes, [(i, i ^ mask) for i in range(4 * count)])

    forward, backward = along(1), along(-1)
    half = count // 2
    own = call(
        pack_kernel,
        rows(packed),
        (a_pattern, g_pattern, curl_tiles, gradient),
        "pack",
        in_specs=[scalars] * 2 + [whole] * 2,
    )
    held = {(0, 0): ("whole", own, 0), (0, 2): ("whole", across(own, 2), 0)}

    def operands_of(pieces):
        buffers, spec = [], {}
        for key, (kind, buffer, begin) in pieces.items():
            if not any(buffer is b for b in buffers):
                buffers.append(buffer)
            spec[key] = (kind, [buffer is b for b in buffers].index(True), begin)
        return buffers, spec

    def exchange(pieces, *over):
        buffers, spec = operands_of(pieces)
        mine, theirs = call(
            collect_kernel,
            [rows(len(pieces) * share)] * 2,
            [*buffers, *over],
            "collect",
            spec,
            compiler_params=limit,
        )
        theirs = across(theirs, 1)
        return {
            (d, m + other): ("share", (mine, theirs)[other], i * share)
            for i, (d, m) in enumerate(spec)
            for other in (0, 1)
        }

    def cut(items, *operands):
        return call(cut_kernel, [rows(crossing)] * len(items), operands, "cut", items, compiler_params=limit)

    for m in (0, 2):
        ahead = back = own
        for step in range(1, half):
            if m == 2 and step == half - 1:
                ahead, back = cut([((0, 0), (1, 1), 0), ((1, 1), (-1, -1), 0)], ahead, back)
            ways = [[(i, j ^ m) if step == 1 else (i, j) for i, j in way] for way in (forward, backward)]
            ahead, back = lax.ppermute(ahead, axes, ways[0]), lax.ppermute(back, axes, ways[1])
            kind = "cross" if m == 2 and step == half - 1 else "whole"
            held[step, m], held[count - step, m] = (kind, ahead, 0), (kind, back, 0)
    split = [pair for pair in forward if pair[0] % 2 == 0] + [pair for pair in backward if pair[0] % 2 == 1]
    straight, diagonal = cut(
        [((0, 1), (1, -1), 0), ((0, 1), (1, -1), 1)], held[half - 1, 0][1], held[half + 1, 0][1]
    )
    held[half, 0] = ("cross", lax.ppermute(straight, axes, split), 0)
    held[half, 2] = ("cross", lax.ppermute(diagonal, axes, [(i, j ^ 2) for i, j in split]), 0)
    early = {key: held[key] for key in held if min(key[0], count - key[0]) <= (3, 2)[key[1] // 2]}
    got = exchange(early)
    distances = [d for d in range(count) if (d, 0) in early and (d, 2) in early]
    buffers, spec = operands_of(got)
    part, g_cols = call(
        early_kernel,
        [
            pltpu.VMEM((row_blocks * BLOCK, 4 * a_rows), jnp.float32),
            pltpu.VMEM((4 * a_rows, out_cols), jnp.bfloat16),
        ],
        buffers,
        "early",
        spec,
        distances,
        scratch_shapes=[pltpu.VMEM((len(distances) * BLOCK, row_blocks * BLOCK), jnp.bfloat16)],
        compiler_params=limit,
    )
    late = {key: piece for key, piece in held.items() if key not in early}
    late.update({(d, m + 1): (kind, across(piece, 1), begin) for (d, m), (kind, piece, begin) in list(late.items())})
    late_distances = [d for d in range(count) if d not in distances]
    last_pieces = {**late, **{key: p for key, p in got.items() if key[0] in late_distances}}
    buffers, spec = operands_of(last_pieces)
    return call(
        product_kernel,
        jax.ShapeDtypeStruct((out_rows, out_cols), jnp.float32),
        buffers + [part, g_cols],
        "product",
        tuple(late),
        spec,
        late_distances,
        scratch_shapes=[
            pltpu.VMEM((4 * a_rows, out_cols), jnp.bfloat16),
            pltpu.VMEM((len(late_distances) * BLOCK, row_blocks * BLOCK), jnp.bfloat16),
            pltpu.VMEM((row_blocks * BLOCK, out_cols), jnp.float32),
            *[pltpu.VMEM((row_blocks * BLOCK, 4 * a_rows), jnp.bfloat16)] * 2,
        ],
        compiler_params=limit,
    )


def gathers(mesh, curl_tiles, gradient):
    count, width = mesh.shape["row"], mesh.shape["col"]
    coarse = gradient.shape[1]
    return (
        width == 4
        and count % 2 == 0
        and curl_tiles.shape[2] // count == BLOCK
        and curl_tiles.shape[1] // width == 32
        and coarse % (width * BLOCK) == 0
        and coarse % (count * 64) == 0
        and 2 * (curl_tiles.size + gradient.size) <= GATHER_LIMIT
    )


def solution(mesh):
    placed = (P(None, "col", "row"), P(("row", "col"), None), P(), P())

    def run(curl_tiles, gradient, a_pattern, g_pattern):
        body = reducing_body
        if gathers(mesh, curl_tiles, gradient):
            body = functools.partial(gathering_body, mesh.shape["row"])
        return jax.shard_map(
            body, mesh=mesh, in_specs=placed, out_specs=P("row", "col"), check_vma=False
        )(curl_tiles, gradient, a_pattern, g_pattern)

    return run
```

```python
import functools

import jax
import jax.numpy as jnp
from jax import lax
from jax.experimental import pallas as pl
from jax.experimental.pallas import tpu as pltpu
from jax.sharding import PartitionSpec as P

BLOCK = 128
GATHER_LIMIT = 8 * 1024 * 1024


def block_hits(position, block_total):
    return (position[:, None] // BLOCK == jnp.arange(block_total, dtype=jnp.int32)[None, :]).astype(
        jnp.float32
    )


def reducing_body(curl_tiles, gradient, a_pattern, g_pattern):
    row_count = lax.axis_size("row")
    row_pos = lax.axis_index("row")
    col_pos = lax.axis_index("col")
    rows_here = curl_tiles.shape[1]
    span_rows = curl_tiles.shape[2]
    fine_blocks = a_pattern.shape[0]
    strided_total = row_count * rows_here
    offsets = jnp.arange(rows_here, dtype=jnp.int32)
    column_index = (
        jnp.arange(row_count, dtype=jnp.int32)[:, None] * span_rows
        + col_pos * rows_here
        + offsets[None, :]
    ).reshape(-1)
    row_index = row_pos * span_rows + jnp.arange(span_rows, dtype=jnp.int32)
    own_index = row_pos * span_rows + col_pos * rows_here + offsets
    picked = jnp.dot(block_hits(row_index, fine_blocks), a_pattern.astype(jnp.float32))
    keep_a = jnp.dot(block_hits(column_index, fine_blocks), picked.T)
    masked_a = curl_tiles.reshape(strided_total, span_rows) * keep_a.astype(jnp.bfloat16)
    keep_g = jnp.dot(block_hits(own_index, fine_blocks), g_pattern.astype(jnp.float32))
    masked_g = gradient * jnp.repeat(keep_g, BLOCK, axis=1).astype(jnp.bfloat16)
    g_group = lax.all_gather(masked_g, "col", axis=0, tiled=True)
    g_strided = lax.all_gather(masked_g, "row", axis=0, tiled=True)
    product_t = lax.psum_scatter(
        lax.dot_general(
            g_strided, masked_a, (((0,), (0,)), ((), ())), preferred_element_type=jnp.float32
        ),
        "col",
        scatter_dimension=0,
        tiled=True,
    )
    return lax.psum_scatter(
        lax.dot_general(
            g_group.astype(jnp.float32),
            product_t,
            (((0,), (1,)), ((), ())),
            precision=lax.Precision.HIGHEST,
            preferred_element_type=jnp.float32,
        ),
        "row",
        scatter_dimension=0,
        tiled=True,
    )


def ring_row(position, count):
    return jnp.where(position < count // 2, 2 * position, 2 * (count - 1 - position) + 1)


def ring_position(row, count):
    return jnp.where(row % 2 == 0, row // 2, count - 1 - row // 2)


def ring_rows(count):
    return list(range(0, count, 2)) + list(range(count - 1, 0, -2))


def layout(count, rows_here, coarse):
    a_rows = count * rows_here
    col_blocks = coarse // 4 // BLOCK
    row_blocks = -(-(coarse // count + 64) // BLOCK)
    crossing = a_rows + (2 * col_blocks + row_blocks) * rows_here
    share = a_rows + (col_blocks + row_blocks) * rows_here
    return a_rows, col_blocks, row_blocks, crossing, share


def first_window(row, count, coarse):
    return (row * (coarse // count)) // BLOCK


def aligned(start):
    return pl.multiple_of(start, 32)


def put(out_ref, at, ref, start, rows):
    out_ref[at : at + rows, :] = ref[pl.ds(start, rows), :]
    return at + rows


def cut_kernel(count, rows_here, coarse, items, *refs):
    a_rows, col_blocks, row_blocks, _, _ = layout(count, rows_here, coarse)
    row, col = lax.axis_index("row"), lax.axis_index("col")
    second = col % 2 == 1
    for (sources, steps, over), out_ref in zip(items, refs[len(refs) - len(items) :]):
        step = jnp.where(second, steps[1] + count, steps[0] + count)
        there = ring_row(lax.rem(ring_position(row, count) + step, count), count)
        half = aligned(a_rows + ((col // 2) ^ over) * (2 * col_blocks * rows_here))
        window = aligned(a_rows + first_window(there, count, coarse) * rows_here)
        at = 0
        for start, n in ((0, a_rows), (half, 2 * col_blocks * rows_here), (window, row_blocks * rows_here)):
            part = refs[sources[0]][pl.ds(start, n), :]
            if sources[1] != sources[0]:
                part = jnp.where(second, refs[sources[1]][pl.ds(start, n), :], part)
            out_ref[at : at + n, :] = part
            at += n


def pack_kernel(count, rows_here, coarse, a_pattern, g_pattern, a_ref, g_ref, out_ref):
    row = lax.axis_index("row")
    a_rows = layout(count, rows_here, coarse)[0]
    for k in range(count):
        out_ref[k * rows_here : (k + 1) * rows_here, :] = jnp.where(a_pattern[row, k] != 0, a_ref[k], 0)
    for j in range(coarse // BLOCK):
        out_ref[a_rows + j * rows_here : a_rows + (j + 1) * rows_here, :] = jnp.where(
            g_pattern[row, j] != 0, g_ref[:, j * BLOCK : (j + 1) * BLOCK], 0
        )


class Piece:
    def __init__(self, kind, ref, begin, sizes):
        self.kind, self.ref, self.begin, self.sizes = kind, ref, begin, sizes

    def tiles(self):
        return self.ref[self.begin : self.begin + self.sizes[0], :]

    def columns(self, rows_here, col):
        a_rows, col_blocks = self.sizes[:2]
        start = self.begin + a_rows
        if self.kind == "whole":
            start = aligned(start + col * (col_blocks * rows_here))
        elif self.kind == "cross":
            start = aligned(start + (col % 2) * (col_blocks * rows_here))
        return start

    def window(self, rows_here, first):
        a_rows, col_blocks = self.sizes[:2]
        start = self.begin + a_rows
        if self.kind == "whole":
            return aligned(start + first * rows_here)
        return start + (2 if self.kind == "cross" else 1) * col_blocks * rows_here


def pieces_of(spec, refs, sizes):
    return {key: Piece(kind, refs[index], begin, sizes) for key, (kind, index, begin) in spec.items()}


def collect_kernel(count, rows_here, coarse, spec, *refs):
    sizes = layout(count, rows_here, coarse)
    a_rows, col_blocks, row_blocks = sizes[:3]
    row, col = lax.axis_index("row"), lax.axis_index("col")
    first = first_window(row, count, coarse)
    for out_ref, owner in ((refs[-2], col), (refs[-1], col ^ 1)):
        at = 0
        for piece in pieces_of(spec, refs, sizes).values():
            at = put(out_ref, at, piece.ref, piece.begin, a_rows)
            at = put(out_ref, at, piece.ref, piece.columns(rows_here, owner), col_blocks * rows_here)
            at = put(out_ref, at, piece.ref, piece.window(rows_here, first), row_blocks * rows_here)


def place_kernel_part(pieces, count, rows_here, coarse, distances, g_cols, g_rows):
    _, col_blocks, row_blocks, _, _ = layout(count, rows_here, coarse)
    a_rows = count * rows_here
    row, col = lax.axis_index("row"), lax.axis_index("col")
    position = ring_position(row, count)
    first = first_window(row, count, coarse)
    for (d, m), piece in pieces.items():
        source = ring_row(lax.rem(position - d + count, count), count)
        if g_cols is not None:
            below = pl.ds(aligned(m * a_rows + source * rows_here), rows_here)
            start = piece.columns(rows_here, col)
            for j in range(col_blocks):
                g_cols[below, j * BLOCK : (j + 1) * BLOCK] = piece.ref[pl.ds(start + j * rows_here, rows_here), :]
        if d in distances:
            below = pl.ds(aligned(distances.index(d) * BLOCK + (col ^ m) * rows_here), rows_here)
            start = piece.window(rows_here, first)
            for j in range(row_blocks):
                g_rows[below, j * BLOCK : (j + 1) * BLOCK] = piece.ref[pl.ds(start + j * rows_here, rows_here), :]


def window_rows(row, count, coarse, g_rows, turned):
    out_rows = coarse // count
    turned[...] = jnp.transpose(g_rows[...])
    shift = pl.multiple_of(row * out_rows - first_window(row, count, coarse) * BLOCK, 64)
    return turned[pl.ds(shift, out_rows), :]


def partial_product(pieces, m, distances, g_turned):
    part = None
    for i in range(0, len(distances), 2):
        pair = distances[i : i + 2]
        tiles = [pieces[d, m].tiles() for d in pair]
        term = lax.dot_general(
            g_turned[:, i * BLOCK : (i + len(pair)) * BLOCK],
            tiles[0] if len(tiles) == 1 else jnp.concatenate(tiles, axis=1),
            (((1,), (1,)), ((), ())),
            preferred_element_type=jnp.float32,
        )
        part = term if part is None else part + term
    return part


def early_kernel(count, rows_here, coarse, spec, distances, *refs):
    part_ref, g_cols, g_rows, turned = refs[-4:]
    sizes = layout(count, rows_here, coarse)
    a_rows = sizes[0]
    pieces = pieces_of(spec, refs, sizes)
    place_kernel_part(pieces, count, rows_here, coarse, distances, g_cols, g_rows)
    g_turned = window_rows(lax.axis_index("row"), count, coarse, g_rows, turned)
    for m in range(4):
        part_ref[:, m * a_rows : (m + 1) * a_rows] = partial_product(pieces, m, distances, g_turned)


def product_kernel(count, rows_here, coarse, late, spec, distances, *refs):
    part_ref, g_early, out_ref, g_cols, g_rows, turned, terms = refs[-7:]
    out_rows = out_ref.shape[0]
    sizes = layout(count, rows_here, coarse)
    a_rows = sizes[0]
    pieces = pieces_of(spec, refs, sizes)
    g_cols[...] = g_early[...]
    place_kernel_part({key: pieces[key] for key in late}, count, rows_here, coarse, distances, g_cols, g_rows)
    rest = {key: piece for key, piece in pieces.items() if key not in late}
    place_kernel_part(rest, count, rows_here, coarse, distances, None, g_rows)
    g_turned = window_rows(lax.axis_index("row"), count, coarse, g_rows, turned)
    for m in range(4):
        columns = slice(m * a_rows, (m + 1) * a_rows)
        part = part_ref[:, columns] + partial_product(pieces, m, distances, g_turned)
        high = part.astype(jnp.bfloat16)
        terms[:out_rows, columns] = high
        terms[out_rows:, columns] = (part - high.astype(jnp.float32)).astype(jnp.bfloat16)
    total = jnp.dot(terms[...], g_cols[...], preferred_element_type=jnp.float32)
    out_ref[...] = total[:out_rows] + total[out_rows:]


def gathering_body(count, curl_tiles, gradient, a_pattern, g_pattern):
    rows_here = curl_tiles.shape[1]
    coarse = gradient.shape[1]
    out_rows, out_cols = coarse // count, coarse // 4
    a_rows, _, row_blocks, crossing, share = layout(count, rows_here, coarse)
    packed = a_rows + coarse // BLOCK * rows_here
    whole, scalars = pl.BlockSpec(memory_space=pltpu.VMEM), pl.BlockSpec(memory_space=pltpu.SMEM)
    limit = pltpu.CompilerParams(vmem_limit_bytes=8 * 1024 * 1024)
    sizes = (count, rows_here, coarse)
    axes = ("row", "col")

    def rows(n):
        return pltpu.VMEM((n, BLOCK), jnp.bfloat16)

    def turning(distances):
        shape = (distances * BLOCK, row_blocks * BLOCK)
        return [pltpu.VMEM(shape, jnp.bfloat16), pltpu.VMEM(shape[::-1], jnp.bfloat16)]

    def call(kernel, out, operands, name, *given, **options):
        return pl.pallas_call(
            functools.partial(kernel, *sizes, *given),
            out_shape=out,
            in_specs=options.pop("in_specs", [whole] * len(operands)),
            out_specs=[whole] * len(out) if isinstance(out, list) else whole,
            name=name,
            **options,
        )(*operands)

    order = ring_rows(count)

    def along(step):
        return [
            (order[p] * 4 + c, order[(p + step) % count] * 4 + c) for p in range(count) for c in range(4)
        ]

    def across(piece, mask):
        return lax.ppermute(piece, axes, [(i, i ^ mask) for i in range(4 * count)])

    forward, backward = along(1), along(-1)
    half = count // 2
    own = call(
        pack_kernel,
        rows(packed),
        (a_pattern, g_pattern, curl_tiles, gradient),
        "pack",
        in_specs=[scalars] * 2 + [whole] * 2,
    )
    held = {(0, 0): ("whole", own, 0), (0, 2): ("whole", across(own, 2), 0)}

    def operands_of(pieces):
        buffers, spec = [], {}
        for key, (kind, buffer, begin) in pieces.items():
            if not any(buffer is b for b in buffers):
                buffers.append(buffer)
            spec[key] = (kind, [buffer is b for b in buffers].index(True), begin)
        return buffers, spec

    def exchange(pieces, *over):
        buffers, spec = operands_of(pieces)
        mine, theirs = call(
            collect_kernel,
            [rows(len(pieces) * share)] * 2,
            [*buffers, *over],
            "collect",
            spec,
            compiler_params=limit,
        )
        theirs = across(theirs, 1)
        return {
            (d, m + other): ("share", (mine, theirs)[other], i * share)
            for i, (d, m) in enumerate(spec)
            for other in (0, 1)
        }

    def cut(items, *operands):
        return call(cut_kernel, [rows(crossing)] * len(items), operands, "cut", items, compiler_params=limit)

    chain = {m: (own, own) for m in (0, 2)}
    for step, m in ((step, m) for step in range(1, half) for m in (0, 2)):
        ahead, back = chain[m]
        kind = "whole"
        if m == 2 and step == half - 1:
            ahead, back = cut([((0, 0), (1, 1), 0), ((1, 1), (-1, -1), 0)], ahead, back)
            kind = "cross"
        ways = [[(i, j ^ m) if step == 1 else (i, j) for i, j in way] for way in (forward, backward)]
        back, ahead = lax.ppermute(back, axes, ways[1]), lax.ppermute(ahead, axes, ways[0])
        chain[m] = ahead, back
        held[step, m], held[count - step, m] = (kind, ahead, 0), (kind, back, 0)
    split = [pair for pair in forward if pair[0] % 2 == 1] + [pair for pair in backward if pair[0] % 2 == 0]
    straight, diagonal = cut(
        [((1, 0), (-1, 1), 0), ((1, 0), (-1, 1), 1)], held[half - 1, 0][1], held[half + 1, 0][1]
    )
    held[half, 0] = ("cross", lax.ppermute(straight, axes, split), 0)
    held[half, 2] = ("cross", lax.ppermute(diagonal, axes, [(i, j ^ 2) for i, j in split]), 0)
    early = {key: held[key] for key in held if min(key[0], count - key[0]) < half - key[1] // 2}
    early = dict(sorted(early.items()))
    got = exchange(early)
    distances = [d for d in range(count) if (d, 0) in early and (d, 2) in early]
    buffers, spec = operands_of(got)
    part, g_cols = call(
        early_kernel,
        [
            pltpu.VMEM((out_rows, 4 * a_rows), jnp.float32),
            pltpu.VMEM((4 * a_rows, out_cols), jnp.bfloat16),
        ],
        buffers,
        "early",
        spec,
        distances,
        scratch_shapes=turning(len(distances)),
        compiler_params=limit,
    )
    late = {key: piece for key, piece in reversed(held.items()) if key not in early}
    late.update({(d, m + 1): (kind, across(piece, 1), begin) for (d, m), (kind, piece, begin) in list(late.items())})
    late_distances = [d for d in range(count) if d not in distances]
    last_pieces = {**late, **{key: p for key, p in got.items() if key[0] in late_distances}}
    buffers, spec = operands_of(last_pieces)
    return call(
        product_kernel,
        jax.ShapeDtypeStruct((out_rows, out_cols), jnp.float32),
        buffers + [part, g_cols],
        "product",
        tuple(late),
        spec,
        late_distances,
        scratch_shapes=[
            pltpu.VMEM((4 * a_rows, out_cols), jnp.bfloat16),
            *turning(len(late_distances)),
            pltpu.VMEM((2 * out_rows, 4 * a_rows), jnp.bfloat16),
        ],
        compiler_params=limit,
    )


def gathers(mesh, curl_tiles, gradient):
    count, width = mesh.shape["row"], mesh.shape["col"]
    coarse = gradient.shape[1]
    return (
        width == 4
        and count % 2 == 0
        and count >= 8
        and curl_tiles.shape[2] // count == BLOCK
        and curl_tiles.shape[1] // width == 32
        and coarse % (width * BLOCK) == 0
        and coarse % (count * 64) == 0
        and 2 * (curl_tiles.size + gradient.size) <= GATHER_LIMIT
    )


def solution(mesh):
    placed = (P(None, "col", "row"), P(("row", "col"), None), P(), P())

    def run(curl_tiles, gradient, a_pattern, g_pattern):
        body = reducing_body
        if gathers(mesh, curl_tiles, gradient):
            body = functools.partial(gathering_body, mesh.shape["row"])
        return jax.shard_map(
            body, mesh=mesh, in_specs=placed, out_specs=P("row", "col"), check_vma=False
        )(curl_tiles, gradient, a_pattern, g_pattern)

    return run
```

```python
import functools

import jax
import jax.numpy as jnp
from jax import lax
from jax.experimental import pallas as pl
from jax.experimental.pallas import tpu as pltpu
from jax.sharding import PartitionSpec as P

BLOCK = 128
GATHER_LIMIT = 8 * 1024 * 1024


def block_hits(position, block_total):
    return (position[:, None] // BLOCK == jnp.arange(block_total, dtype=jnp.int32)[None, :]).astype(
        jnp.float32
    )


def reducing_body(curl_tiles, gradient, a_pattern, g_pattern):
    row_count = lax.axis_size("row")
    row_pos = lax.axis_index("row")
    col_pos = lax.axis_index("col")
    rows_here = curl_tiles.shape[1]
    span_rows = curl_tiles.shape[2]
    fine_blocks = a_pattern.shape[0]
    strided_total = row_count * rows_here
    offsets = jnp.arange(rows_here, dtype=jnp.int32)
    column_index = (
        jnp.arange(row_count, dtype=jnp.int32)[:, None] * span_rows
        + col_pos * rows_here
        + offsets[None, :]
    ).reshape(-1)
    row_index = row_pos * span_rows + jnp.arange(span_rows, dtype=jnp.int32)
    own_index = row_pos * span_rows + col_pos * rows_here + offsets
    picked = jnp.dot(block_hits(row_index, fine_blocks), a_pattern.astype(jnp.float32))
    keep_a = jnp.dot(block_hits(column_index, fine_blocks), picked.T)
    masked_a = curl_tiles.reshape(strided_total, span_rows) * keep_a.astype(jnp.bfloat16)
    keep_g = jnp.dot(block_hits(own_index, fine_blocks), g_pattern.astype(jnp.float32))
    masked_g = gradient * jnp.repeat(keep_g, BLOCK, axis=1).astype(jnp.bfloat16)
    g_group = lax.all_gather(masked_g, "col", axis=0, tiled=True)
    g_strided = lax.all_gather(masked_g, "row", axis=0, tiled=True)
    product_t = lax.psum_scatter(
        lax.dot_general(
            g_strided, masked_a, (((0,), (0,)), ((), ())), preferred_element_type=jnp.float32
        ),
        "col",
        scatter_dimension=0,
        tiled=True,
    )
    return lax.psum_scatter(
        lax.dot_general(
            g_group.astype(jnp.float32),
            product_t,
            (((0,), (1,)), ((), ())),
            precision=lax.Precision.HIGHEST,
            preferred_element_type=jnp.float32,
        ),
        "row",
        scatter_dimension=0,
        tiled=True,
    )


def ring_row(position, count):
    return jnp.where(position < count // 2, 2 * position, 2 * (count - 1 - position) + 1)


def ring_position(row, count):
    return jnp.where(row % 2 == 0, row // 2, count - 1 - row // 2)


def ring_rows(count):
    return list(range(0, count, 2)) + list(range(count - 1, 0, -2))


def layout(count, rows_here, coarse):
    a_rows = count * rows_here
    col_blocks = coarse // 4 // BLOCK
    row_blocks = -(-(coarse // count + 64) // BLOCK)
    crossing = a_rows + (2 * col_blocks + row_blocks) * rows_here
    share = a_rows + (col_blocks + row_blocks) * rows_here
    return a_rows, col_blocks, row_blocks, crossing, share


def first_window(row, count, coarse):
    return (row * (coarse // count)) // BLOCK


def aligned(start):
    return pl.multiple_of(start, 32)


def put(out_ref, at, ref, start, rows):
    out_ref[at : at + rows, :] = ref[pl.ds(start, rows), :]
    return at + rows


def cut_kernel(count, rows_here, coarse, items, *refs):
    a_rows, col_blocks, row_blocks, _, _ = layout(count, rows_here, coarse)
    row, col = lax.axis_index("row"), lax.axis_index("col")
    second = col % 2 == 1
    for (sources, steps, over), out_ref in zip(items, refs[len(refs) - len(items) :]):
        step = jnp.where(second, steps[1] + count, steps[0] + count)
        there = ring_row(lax.rem(ring_position(row, count) + step, count), count)
        half = aligned(a_rows + ((col // 2) ^ over) * (2 * col_blocks * rows_here))
        window = aligned(a_rows + first_window(there, count, coarse) * rows_here)
        at = 0
        for start, n in ((0, a_rows), (half, 2 * col_blocks * rows_here), (window, row_blocks * rows_here)):
            part = refs[sources[0]][pl.ds(start, n), :]
            if sources[1] != sources[0]:
                part = jnp.where(second, refs[sources[1]][pl.ds(start, n), :], part)
            out_ref[at : at + n, :] = part
            at += n


def pack_kernel(count, rows_here, coarse, a_pattern, g_pattern, a_ref, g_ref, out_ref, cross_ref):
    row = lax.axis_index("row")
    a_rows = layout(count, rows_here, coarse)[0]
    for k in range(count):
        out_ref[k * rows_here : (k + 1) * rows_here, :] = jnp.where(a_pattern[row, k] != 0, a_ref[k], 0)
    for j in range(coarse // BLOCK):
        out_ref[a_rows + j * rows_here : a_rows + (j + 1) * rows_here, :] = jnp.where(
            g_pattern[row, j] != 0, g_ref[:, j * BLOCK : (j + 1) * BLOCK], 0
        )
    cut_kernel(count, rows_here, coarse, [((0, 0), (0, 0), 1)], out_ref, cross_ref)


class Piece:
    def __init__(self, kind, ref, begin, sizes):
        self.kind, self.ref, self.begin, self.sizes = kind, ref, begin, sizes

    def tiles(self):
        return self.ref[self.begin : self.begin + self.sizes[0], :]

    def columns(self, rows_here, col):
        a_rows, col_blocks = self.sizes[:2]
        start = self.begin + a_rows
        if self.kind == "whole":
            start = aligned(start + col * (col_blocks * rows_here))
        elif self.kind == "cross":
            start = aligned(start + (col % 2) * (col_blocks * rows_here))
        return start

    def window(self, rows_here, first):
        a_rows, col_blocks = self.sizes[:2]
        start = self.begin + a_rows
        if self.kind == "whole":
            return aligned(start + first * rows_here)
        return start + (2 if self.kind == "cross" else 1) * col_blocks * rows_here


def pieces_of(spec, refs, sizes):
    return {key: Piece(kind, refs[index], begin, sizes) for key, (kind, index, begin) in spec.items()}


def collect_kernel(count, rows_here, coarse, spec, *refs):
    sizes = layout(count, rows_here, coarse)
    a_rows, col_blocks, row_blocks = sizes[:3]
    row, col = lax.axis_index("row"), lax.axis_index("col")
    first = first_window(row, count, coarse)
    for out_ref, owner in ((refs[-2], col), (refs[-1], col ^ 1)):
        at = 0
        for piece in pieces_of(spec, refs, sizes).values():
            at = put(out_ref, at, piece.ref, piece.begin, a_rows)
            at = put(out_ref, at, piece.ref, piece.columns(rows_here, owner), col_blocks * rows_here)
            at = put(out_ref, at, piece.ref, piece.window(rows_here, first), row_blocks * rows_here)


def place_kernel_part(pieces, count, rows_here, coarse, distances, g_cols, g_rows):
    _, col_blocks, row_blocks, _, _ = layout(count, rows_here, coarse)
    a_rows = count * rows_here
    row, col = lax.axis_index("row"), lax.axis_index("col")
    position = ring_position(row, count)
    first = first_window(row, count, coarse)
    for (d, m), piece in pieces.items():
        source = ring_row(lax.rem(position - d + count, count), count)
        if g_cols is not None:
            below = pl.ds(aligned(m * a_rows + source * rows_here), rows_here)
            start = piece.columns(rows_here, col)
            for j in range(col_blocks):
                g_cols[below, j * BLOCK : (j + 1) * BLOCK] = piece.ref[pl.ds(start + j * rows_here, rows_here), :]
        if d in distances:
            below = pl.ds(aligned(distances.index(d) * BLOCK + (col ^ m) * rows_here), rows_here)
            start = piece.window(rows_here, first)
            for j in range(row_blocks):
                g_rows[below, j * BLOCK : (j + 1) * BLOCK] = piece.ref[pl.ds(start + j * rows_here, rows_here), :]


def window_rows(row, count, coarse, g_rows, turned):
    out_rows = coarse // count
    turned[...] = jnp.transpose(g_rows[...])
    shift = pl.multiple_of(row * out_rows - first_window(row, count, coarse) * BLOCK, 64)
    return turned[pl.ds(shift, out_rows), :]


def partial_product(pieces, m, distances, g_turned):
    part = None
    for i in range(0, len(distances), 2):
        pair = distances[i : i + 2]
        tiles = [pieces[d, m].tiles() for d in pair]
        term = lax.dot_general(
            g_turned[:, i * BLOCK : (i + len(pair)) * BLOCK],
            tiles[0] if len(tiles) == 1 else jnp.concatenate(tiles, axis=1),
            (((1,), (1,)), ((), ())),
            preferred_element_type=jnp.float32,
        )
        part = term if part is None else part + term
    return part


def early_kernel(count, rows_here, coarse, spec, distances, *refs):
    part_ref, g_cols, g_rows, turned = refs[-4:]
    sizes = layout(count, rows_here, coarse)
    a_rows = sizes[0]
    pieces = pieces_of(spec, refs, sizes)
    place_kernel_part(pieces, count, rows_here, coarse, distances, g_cols, g_rows)
    g_turned = window_rows(lax.axis_index("row"), count, coarse, g_rows, turned)
    for m in range(4):
        part_ref[:, m * a_rows : (m + 1) * a_rows] = partial_product(pieces, m, distances, g_turned)


def product_kernel(count, rows_here, coarse, late, spec, distances, *refs):
    part_ref, g_early, out_ref, g_cols, g_rows, turned, terms, block, sent = refs[-9:]
    out_rows = out_ref.shape[0]
    sizes = layout(count, rows_here, coarse)
    a_rows = sizes[0]
    pieces = pieces_of(spec, refs, sizes)
    g_cols[...] = g_early[...]
    place_kernel_part({key: pieces[key] for key in late}, count, rows_here, coarse, distances, g_cols, g_rows)
    rest = {key: piece for key, piece in pieces.items() if key not in late}
    place_kernel_part(rest, count, rows_here, coarse, distances, None, g_rows)
    g_turned = window_rows(lax.axis_index("row"), count, coarse, g_rows, turned)
    for m in range(4):
        columns = slice(m * a_rows, (m + 1) * a_rows)
        part = part_ref[:, columns] + partial_product(pieces, m, distances, g_turned)
        high = part.astype(jnp.bfloat16)
        terms[:out_rows, columns] = high
        terms[out_rows:, columns] = (part - high.astype(jnp.float32)).astype(jnp.bfloat16)
    copies = []
    out_cols = out_ref.shape[1]
    for i, (first, last) in enumerate(((0, out_cols - BLOCK), (out_cols - BLOCK, out_cols))):
        total = jnp.dot(terms[...], g_cols[:, first:last], preferred_element_type=jnp.float32)
        block[:, first:last] = total[:out_rows] + total[out_rows:]
        columns = pl.ds(first, last - first)
        copies.append(pltpu.make_async_copy(block.at[:, columns], out_ref.at[:, columns], sent.at[i]))
        copies[-1].start()
    for copy in copies:
        copy.wait()


def gathering_body(count, curl_tiles, gradient, a_pattern, g_pattern):
    rows_here = curl_tiles.shape[1]
    coarse = gradient.shape[1]
    out_rows, out_cols = coarse // count, coarse // 4
    a_rows, _, row_blocks, crossing, share = layout(count, rows_here, coarse)
    packed = a_rows + coarse // BLOCK * rows_here
    whole, scalars = pl.BlockSpec(memory_space=pltpu.VMEM), pl.BlockSpec(memory_space=pltpu.SMEM)
    limit = pltpu.CompilerParams(vmem_limit_bytes=8 * 1024 * 1024)
    sizes = (count, rows_here, coarse)
    axes = ("row", "col")

    def rows(n):
        return pltpu.VMEM((n, BLOCK), jnp.bfloat16)

    def turning(distances):
        shape = (distances * BLOCK, row_blocks * BLOCK)
        return [pltpu.VMEM(shape, jnp.bfloat16), pltpu.VMEM(shape[::-1], jnp.bfloat16)]

    def call(kernel, out, operands, name, *given, **options):
        return pl.pallas_call(
            functools.partial(kernel, *sizes, *given),
            out_shape=out,
            in_specs=options.pop("in_specs", [whole] * len(operands)),
            out_specs=options.pop("out_specs", [whole] * len(out) if isinstance(out, list) else whole),
            name=name,
            **options,
        )(*operands)

    order = ring_rows(count)

    def along(step):
        return [
            (order[p] * 4 + c, order[(p + step) % count] * 4 + c) for p in range(count) for c in range(4)
        ]

    def across(piece, mask):
        return lax.ppermute(piece, axes, [(i, i ^ mask) for i in range(4 * count)])

    forward, backward = along(1), along(-1)
    half = count // 2
    own, cross = call(
        pack_kernel,
        [rows(packed), rows(crossing)],
        (a_pattern, g_pattern, curl_tiles, gradient),
        "pack",
        in_specs=[scalars] * 2 + [whole] * 2,
    )
    held = {(0, 0): ("whole", own, 0), (0, 2): ("cross", across(cross, 2), 0)}

    def operands_of(pieces):
        buffers, spec = [], {}
        for key, (kind, buffer, begin) in pieces.items():
            if not any(buffer is b for b in buffers):
                buffers.append(buffer)
            spec[key] = (kind, [buffer is b for b in buffers].index(True), begin)
        return buffers, spec

    def exchange(pieces, *over):
        buffers, spec = operands_of(pieces)
        mine, theirs = call(
            collect_kernel,
            [rows(len(pieces) * share)] * 2,
            [*buffers, *over],
            "collect",
            spec,
            compiler_params=limit,
        )
        theirs = across(theirs, 1)
        return {
            (d, m + other): ("share", (mine, theirs)[other], i * share)
            for i, (d, m) in enumerate(spec)
            for other in (0, 1)
        }

    def cut(items, *operands):
        return call(cut_kernel, [rows(crossing)] * len(items), operands, "cut", items, compiler_params=limit)

    chain = {m: (own, own) for m in (0, 2)}
    for m, step in ((m, step) for m in (0, 2) for step in range(1, half)):
        ahead, back = chain[m]
        kind = "whole"
        if m == 2 and step == half - 1:
            ahead, back = cut([((0, 0), (1, 1), 0), ((1, 1), (-1, -1), 0)], ahead, back)
            kind = "cross"
        ways = [[(i, j ^ m) if step == 1 else (i, j) for i, j in way] for way in (forward, backward)]
        ahead, back = chain[m] = lax.ppermute(ahead, axes, ways[0]), lax.ppermute(back, axes, ways[1])
        held[step, m], held[count - step, m] = (kind, ahead, 0), (kind, back, 0)
    split = [pair for pair in forward if pair[0] % 2 == 1] + [pair for pair in backward if pair[0] % 2 == 0]
    straight, diagonal = cut(
        [((1, 0), (-1, 1), 0), ((1, 0), (-1, 1), 1)], held[half - 1, 0][1], held[half + 1, 0][1]
    )
    held[half, 0] = ("cross", lax.ppermute(straight, axes, split), 0)
    held[half, 2] = ("cross", lax.ppermute(diagonal, axes, [(i, j ^ 2) for i, j in split]), 0)
    early = {key: held[key] for key in held if min(key[0], count - key[0]) < half - key[1] // 2}
    early = dict(sorted(early.items()))
    got = exchange(early)
    distances = [d for d in range(count) if (d, 0) in early and (d, 2) in early]
    buffers, spec = operands_of(got)
    part, g_cols = call(
        early_kernel,
        [
            pltpu.VMEM((out_rows, 4 * a_rows), jnp.float32),
            pltpu.VMEM((4 * a_rows, out_cols), jnp.bfloat16),
        ],
        buffers,
        "early",
        spec,
        distances,
        scratch_shapes=turning(len(distances)),
        compiler_params=limit,
    )
    late = {key: piece for key, piece in reversed(held.items()) if key not in early}
    late.update({(d, m + 1): (kind, across(piece, 1), begin) for (d, m), (kind, piece, begin) in list(late.items())})
    late_distances = [d for d in range(count) if d not in distances]
    last_pieces = {**late, **{key: p for key, p in got.items() if key[0] in late_distances}}
    buffers, spec = operands_of(last_pieces)
    return call(
        product_kernel,
        jax.ShapeDtypeStruct((out_rows, out_cols), jnp.float32),
        buffers + [part, g_cols],
        "product",
        tuple(late),
        spec,
        late_distances,
        scratch_shapes=[
            pltpu.VMEM((4 * a_rows, out_cols), jnp.bfloat16),
            *turning(len(late_distances)),
            pltpu.VMEM((2 * out_rows, 4 * a_rows), jnp.bfloat16),
            pltpu.VMEM((out_rows, out_cols), jnp.float32),
            pltpu.SemaphoreType.DMA((2,)),
        ],
        out_specs=pl.BlockSpec(memory_space=pl.ANY),
        compiler_params=limit,
    )


def gathers(mesh, curl_tiles, gradient):
    count, width = mesh.shape["row"], mesh.shape["col"]
    coarse = gradient.shape[1]
    return (
        width == 4
        and count % 2 == 0
        and count >= 8
        and curl_tiles.shape[2] // count == BLOCK
        and curl_tiles.shape[1] // width == 32
        and coarse % (width * BLOCK) == 0
        and coarse % (count * 64) == 0
        and 2 * (curl_tiles.size + gradient.size) <= GATHER_LIMIT
    )


def solution(mesh):
    placed = (P(None, "col", "row"), P(("row", "col"), None), P(), P())

    def run(curl_tiles, gradient, a_pattern, g_pattern):
        body = reducing_body
        if gathers(mesh, curl_tiles, gradient):
            body = functools.partial(gathering_body, mesh.shape["row"])
        return jax.shard_map(
            body, mesh=mesh, in_specs=placed, out_specs=P("row", "col"), check_vma=False
        )(curl_tiles, gradient, a_pattern, g_pattern)

    return run
```

```python
import functools

import jax
import jax.numpy as jnp
from jax import lax
from jax.experimental import pallas as pl
from jax.experimental.pallas import tpu as pltpu
from jax.sharding import PartitionSpec as P

BLOCK = 128
GATHER_LIMIT = 8 * 1024 * 1024


def block_hits(position, block_total):
    return (position[:, None] // BLOCK == jnp.arange(block_total, dtype=jnp.int32)[None, :]).astype(
        jnp.float32
    )


def reducing_body(curl_tiles, gradient, a_pattern, g_pattern):
    row_count = lax.axis_size("row")
    row_pos = lax.axis_index("row")
    col_pos = lax.axis_index("col")
    rows_here = curl_tiles.shape[1]
    span_rows = curl_tiles.shape[2]
    fine_blocks = a_pattern.shape[0]
    strided_total = row_count * rows_here
    offsets = jnp.arange(rows_here, dtype=jnp.int32)
    column_index = (
        jnp.arange(row_count, dtype=jnp.int32)[:, None] * span_rows
        + col_pos * rows_here
        + offsets[None, :]
    ).reshape(-1)
    row_index = row_pos * span_rows + jnp.arange(span_rows, dtype=jnp.int32)
    own_index = row_pos * span_rows + col_pos * rows_here + offsets
    picked = jnp.dot(block_hits(row_index, fine_blocks), a_pattern.astype(jnp.float32))
    keep_a = jnp.dot(block_hits(column_index, fine_blocks), picked.T)
    masked_a = curl_tiles.reshape(strided_total, span_rows) * keep_a.astype(jnp.bfloat16)
    keep_g = jnp.dot(block_hits(own_index, fine_blocks), g_pattern.astype(jnp.float32))
    masked_g = gradient * jnp.repeat(keep_g, BLOCK, axis=1).astype(jnp.bfloat16)
    g_group = lax.all_gather(masked_g, "col", axis=0, tiled=True)
    g_strided = lax.all_gather(masked_g, "row", axis=0, tiled=True)
    product_t = lax.psum_scatter(
        lax.dot_general(
            g_strided, masked_a, (((0,), (0,)), ((), ())), preferred_element_type=jnp.float32
        ),
        "col",
        scatter_dimension=0,
        tiled=True,
    )
    return lax.psum_scatter(
        lax.dot_general(
            g_group.astype(jnp.float32),
            product_t,
            (((0,), (1,)), ((), ())),
            precision=lax.Precision.HIGHEST,
            preferred_element_type=jnp.float32,
        ),
        "row",
        scatter_dimension=0,
        tiled=True,
    )


def ring_row(position, count):
    return jnp.where(position < count // 2, 2 * position, 2 * (count - 1 - position) + 1)


def ring_position(row, count):
    return jnp.where(row % 2 == 0, row // 2, count - 1 - row // 2)


def ring_rows(count):
    return list(range(0, count, 2)) + list(range(count - 1, 0, -2))


def layout(count, rows_here, coarse):
    a_rows = count * rows_here
    col_blocks = coarse // 4 // BLOCK
    row_blocks = -(-(coarse // count + 64) // BLOCK)
    crossing = a_rows + (2 * col_blocks + row_blocks) * rows_here
    share = a_rows + (col_blocks + row_blocks) * rows_here
    return a_rows, col_blocks, row_blocks, crossing, share


def first_window(row, count, coarse):
    return (row * (coarse // count)) // BLOCK


def aligned(start):
    return pl.multiple_of(start, 32)


def put(out_ref, at, ref, start, rows):
    out_ref[at : at + rows, :] = ref[pl.ds(start, rows), :]
    return at + rows


def cut_kernel(count, rows_here, coarse, items, *refs):
    a_rows, col_blocks, row_blocks, _, _ = layout(count, rows_here, coarse)
    row, col = lax.axis_index("row"), lax.axis_index("col")
    second = col % 2 == 1
    for (sources, steps, over), out_ref in zip(items, refs[len(refs) - len(items) :]):
        step = jnp.where(second, steps[1] + count, steps[0] + count)
        there = ring_row(lax.rem(ring_position(row, count) + step, count), count)
        half = aligned(a_rows + ((col // 2) ^ over) * (2 * col_blocks * rows_here))
        window = aligned(a_rows + first_window(there, count, coarse) * rows_here)
        at = 0
        for start, n in ((0, a_rows), (half, 2 * col_blocks * rows_here), (window, row_blocks * rows_here)):
            part = refs[sources[0]][pl.ds(start, n), :]
            if sources[1] != sources[0]:
                part = jnp.where(second, refs[sources[1]][pl.ds(start, n), :], part)
            out_ref[at : at + n, :] = part
            at += n


def pack_kernel(count, rows_here, coarse, a_pattern, g_pattern, a_ref, g_ref, out_ref, cross_ref):
    row = lax.axis_index("row")
    a_rows = layout(count, rows_here, coarse)[0]
    for k in range(count):
        out_ref[k * rows_here : (k + 1) * rows_here, :] = jnp.where(a_pattern[row, k] != 0, a_ref[k], 0)
    for j in range(coarse // BLOCK):
        out_ref[a_rows + j * rows_here : a_rows + (j + 1) * rows_here, :] = jnp.where(
            g_pattern[row, j] != 0, g_ref[:, j * BLOCK : (j + 1) * BLOCK], 0
        )
    cut_kernel(count, rows_here, coarse, [((0, 0), (0, 0), 1)], out_ref, cross_ref)


class Piece:
    def __init__(self, kind, ref, begin, sizes):
        self.kind, self.ref, self.begin, self.sizes = kind, ref, begin, sizes

    def tiles(self):
        return self.ref[self.begin : self.begin + self.sizes[0], :]

    def columns(self, rows_here, col):
        a_rows, col_blocks = self.sizes[:2]
        start = self.begin + a_rows
        if self.kind == "whole":
            start = aligned(start + col * (col_blocks * rows_here))
        elif self.kind == "cross":
            start = aligned(start + (col % 2) * (col_blocks * rows_here))
        return start

    def window(self, rows_here, first):
        a_rows, col_blocks = self.sizes[:2]
        start = self.begin + a_rows
        if self.kind == "whole":
            return aligned(start + first * rows_here)
        return start + (2 if self.kind == "cross" else 1) * col_blocks * rows_here


def pieces_of(spec, refs, sizes):
    return {key: Piece(kind, refs[index], begin, sizes) for key, (kind, index, begin) in spec.items()}


def collect_kernel(count, rows_here, coarse, spec, *refs):
    sizes = layout(count, rows_here, coarse)
    a_rows, col_blocks, row_blocks = sizes[:3]
    row, col = lax.axis_index("row"), lax.axis_index("col")
    first = first_window(row, count, coarse)
    for out_ref, owner in ((refs[-2], col), (refs[-1], col ^ 1)):
        at = 0
        for piece in pieces_of(spec, refs, sizes).values():
            at = put(out_ref, at, piece.ref, piece.begin, a_rows)
            at = put(out_ref, at, piece.ref, piece.columns(rows_here, owner), col_blocks * rows_here)
            at = put(out_ref, at, piece.ref, piece.window(rows_here, first), row_blocks * rows_here)


def place_kernel_part(pieces, count, rows_here, coarse, distances, g_cols, g_rows):
    _, col_blocks, row_blocks, _, _ = layout(count, rows_here, coarse)
    a_rows = count * rows_here
    row, col = lax.axis_index("row"), lax.axis_index("col")
    position = ring_position(row, count)
    first = first_window(row, count, coarse)
    for (d, m), piece in pieces.items():
        source = ring_row(lax.rem(position - d + count, count), count)
        if g_cols is not None:
            below = pl.ds(aligned(m * a_rows + source * rows_here), rows_here)
            start = piece.columns(rows_here, col)
            for j in range(col_blocks):
                g_cols[below, j * BLOCK : (j + 1) * BLOCK] = piece.ref[pl.ds(start + j * rows_here, rows_here), :]
        if d in distances:
            below = pl.ds(aligned(distances.index(d) * BLOCK + (col ^ m) * rows_here), rows_here)
            start = piece.window(rows_here, first)
            for j in range(row_blocks):
                g_rows[below, j * BLOCK : (j + 1) * BLOCK] = piece.ref[pl.ds(start + j * rows_here, rows_here), :]


def window_rows(row, count, coarse, g_rows, turned):
    out_rows = coarse // count
    turned[...] = jnp.transpose(g_rows[...])
    shift = pl.multiple_of(row * out_rows - first_window(row, count, coarse) * BLOCK, 64)
    return turned[pl.ds(shift, out_rows), :]


def partial_product(pieces, m, distances, g_turned):
    part = None
    for i in range(0, len(distances), 2):
        pair = distances[i : i + 2]
        tiles = [pieces[d, m].tiles() for d in pair]
        term = lax.dot_general(
            g_turned[:, i * BLOCK : (i + len(pair)) * BLOCK],
            tiles[0] if len(tiles) == 1 else jnp.concatenate(tiles, axis=1),
            (((1,), (1,)), ((), ())),
            preferred_element_type=jnp.float32,
        )
        part = term if part is None else part + term
    return part


def early_kernel(count, rows_here, coarse, spec, distances, *refs):
    part_ref, g_cols, g_rows, turned = refs[-4:]
    sizes = layout(count, rows_here, coarse)
    a_rows = sizes[0]
    pieces = pieces_of(spec, refs, sizes)
    place_kernel_part(pieces, count, rows_here, coarse, distances, g_cols, g_rows)
    g_turned = window_rows(lax.axis_index("row"), count, coarse, g_rows, turned)
    for m in range(4):
        part_ref[:, m * a_rows : (m + 1) * a_rows] = partial_product(pieces, m, distances, g_turned)


def product_kernel(count, rows_here, coarse, late, spec, distances, *refs):
    part_ref, g_early, out_ref, g_cols, g_rows, turned, terms, block, sent = refs[-9:]
    out_rows = out_ref.shape[0]
    sizes = layout(count, rows_here, coarse)
    a_rows = sizes[0]
    pieces = pieces_of(spec, refs, sizes)
    g_cols[...] = g_early[...]
    place_kernel_part({key: pieces[key] for key in late}, count, rows_here, coarse, distances, g_cols, g_rows)
    rest = {key: piece for key, piece in pieces.items() if key not in late}
    place_kernel_part(rest, count, rows_here, coarse, distances, None, g_rows)
    g_turned = window_rows(lax.axis_index("row"), count, coarse, g_rows, turned)
    for m in range(4):
        columns = slice(m * a_rows, (m + 1) * a_rows)
        part = part_ref[:, columns] + partial_product(pieces, m, distances, g_turned)
        high = part.astype(jnp.bfloat16)
        terms[:out_rows, columns] = high
        terms[out_rows:, columns] = (part - high.astype(jnp.float32)).astype(jnp.bfloat16)
    copies = []
    out_cols = out_ref.shape[1]
    for i, (first, last) in enumerate(((0, out_cols - BLOCK), (out_cols - BLOCK, out_cols))):
        total = jnp.dot(terms[...], g_cols[:, first:last], preferred_element_type=jnp.float32)
        block[:, first:last] = total[:out_rows] + total[out_rows:]
        columns = pl.ds(first, last - first)
        copies.append(pltpu.make_async_copy(block.at[:, columns], out_ref.at[:, columns], sent.at[i]))
        copies[-1].start()
    for copy in copies:
        copy.wait()


def gathering_body(count, curl_tiles, gradient, a_pattern, g_pattern):
    rows_here = curl_tiles.shape[1]
    coarse = gradient.shape[1]
    out_rows, out_cols = coarse // count, coarse // 4
    a_rows, _, row_blocks, crossing, share = layout(count, rows_here, coarse)
    packed = a_rows + coarse // BLOCK * rows_here
    whole, scalars = pl.BlockSpec(memory_space=pltpu.VMEM), pl.BlockSpec(memory_space=pltpu.SMEM)
    limit = pltpu.CompilerParams(vmem_limit_bytes=8 * 1024 * 1024)
    sizes = (count, rows_here, coarse)
    axes = ("row", "col")

    def rows(n):
        return pltpu.VMEM((n, BLOCK), jnp.bfloat16)

    def turning(distances):
        shape = (distances * BLOCK, row_blocks * BLOCK)
        return [pltpu.VMEM(shape, jnp.bfloat16), pltpu.VMEM(shape[::-1], jnp.bfloat16)]

    def call(kernel, out, operands, name, *given, **options):
        return pl.pallas_call(
            functools.partial(kernel, *sizes, *given),
            out_shape=out,
            in_specs=options.pop("in_specs", [whole] * len(operands)),
            out_specs=options.pop("out_specs", [whole] * len(out) if isinstance(out, list) else whole),
            name=name,
            **options,
        )(*operands)

    order = ring_rows(count)

    def along(step):
        return [
            (order[p] * 4 + c, order[(p + step) % count] * 4 + c) for p in range(count) for c in range(4)
        ]

    def across(piece, mask):
        return lax.ppermute(piece, axes, [(i, i ^ mask) for i in range(4 * count)])

    forward, backward = along(1), along(-1)
    half = count // 2
    own, cross = call(
        pack_kernel,
        [rows(packed), rows(crossing)],
        (a_pattern, g_pattern, curl_tiles, gradient),
        "pack",
        in_specs=[scalars] * 2 + [whole] * 2,
    )
    held = {(0, 0): ("whole", own, 0)}

    def operands_of(pieces):
        buffers, spec = [], {}
        for key, (kind, buffer, begin) in pieces.items():
            if not any(buffer is b for b in buffers):
                buffers.append(buffer)
            spec[key] = (kind, [buffer is b for b in buffers].index(True), begin)
        return buffers, spec

    def exchange(pieces, *over):
        buffers, spec = operands_of(pieces)
        mine, theirs = call(
            collect_kernel,
            [rows(len(pieces) * share)] * 2,
            [*buffers, *over],
            "collect",
            spec,
            compiler_params=limit,
        )
        theirs = across(theirs, 1)
        return {
            (d, m + other): ("share", (mine, theirs)[other], i * share)
            for i, (d, m) in enumerate(spec)
            for other in (0, 1)
        }

    def cut(items, *operands):
        return call(cut_kernel, [rows(crossing)] * len(items), operands, "cut", items, compiler_params=limit)

    chain = {m: (own, own) for m in (0, 2)}
    for m, step in ((m, step) for m in (0, 2) for step in range(1, half)):
        ahead, back = chain[m]
        kind = "whole"
        if m == 2 and step == half - 1:
            ahead, back = cut([((0, 0), (1, 1), 0), ((1, 1), (-1, -1), 0)], ahead, back)
            kind = "cross"
        ways = [[(i, j ^ m) if step == 1 else (i, j) for i, j in way] for way in (forward, backward)]
        ahead, back = chain[m] = lax.ppermute(ahead, axes, ways[0]), lax.ppermute(back, axes, ways[1])
        held[step, m], held[count - step, m] = (kind, ahead, 0), (kind, back, 0)
    split = [pair for pair in forward if pair[0] % 2 == 1] + [pair for pair in backward if pair[0] % 2 == 0]
    straight, diagonal = cut(
        [((1, 0), (-1, 1), 0), ((1, 0), (-1, 1), 1)], held[half - 1, 0][1], held[half + 1, 0][1]
    )
    held[half, 0] = ("cross", lax.ppermute(straight, axes, split), 0)
    held[half, 2] = ("cross", lax.ppermute(diagonal, axes, [(i, j ^ 2) for i, j in split]), 0)
    held[0, 2] = ("cross", across(cross, 2), 0)
    early = {key: held[key] for key in held if min(key[0], count - key[0]) < half - key[1] // 2}
    got = exchange(early)
    distances = [d for d in range(count) if (d, 0) in early and (d, 2) in early]
    buffers, spec = operands_of(got)
    part, g_cols = call(
        early_kernel,
        [
            pltpu.VMEM((out_rows, 4 * a_rows), jnp.float32),
            pltpu.VMEM((4 * a_rows, out_cols), jnp.bfloat16),
        ],
        buffers,
        "early",
        spec,
        distances,
        scratch_shapes=turning(len(distances)),
        compiler_params=limit,
    )
    late = {key: piece for key, piece in reversed(held.items()) if key not in early}
    late.update({(d, m + 1): (kind, across(piece, 1), begin) for (d, m), (kind, piece, begin) in list(late.items())})
    late_distances = [d for d in range(count) if d not in distances]
    last_pieces = {**late, **{key: p for key, p in got.items() if key[0] in late_distances}}
    buffers, spec = operands_of(last_pieces)
    return call(
        product_kernel,
        jax.ShapeDtypeStruct((out_rows, out_cols), jnp.float32),
        buffers + [part, g_cols],
        "product",
        tuple(late),
        spec,
        late_distances,
        scratch_shapes=[
            pltpu.VMEM((4 * a_rows, out_cols), jnp.bfloat16),
            *turning(len(late_distances)),
            pltpu.VMEM((2 * out_rows, 4 * a_rows), jnp.bfloat16),
            pltpu.VMEM((out_rows, out_cols), jnp.float32),
            pltpu.SemaphoreType.DMA((2,)),
        ],
        out_specs=pl.BlockSpec(memory_space=pl.ANY),
        compiler_params=limit,
    )


def gathers(mesh, curl_tiles, gradient):
    count, width = mesh.shape["row"], mesh.shape["col"]
    coarse = gradient.shape[1]
    return (
        width == 4
        and count % 2 == 0
        and count >= 8
        and curl_tiles.shape[2] // count == BLOCK
        and curl_tiles.shape[1] // width == 32
        and coarse % (width * BLOCK) == 0
        and coarse % (count * 64) == 0
        and 2 * (curl_tiles.size + gradient.size) <= GATHER_LIMIT
    )


def solution(mesh):
    placed = (P(None, "col", "row"), P(("row", "col"), None), P(), P())

    def run(curl_tiles, gradient, a_pattern, g_pattern):
        body = reducing_body
        if gathers(mesh, curl_tiles, gradient):
            body = functools.partial(gathering_body, mesh.shape["row"])
        return jax.shard_map(
            body, mesh=mesh, in_specs=placed, out_specs=P("row", "col"), check_vma=False
        )(curl_tiles, gradient, a_pattern, g_pattern)

    return run
```

```python
import functools

import jax
import jax.numpy as jnp
from jax import lax
from jax.experimental import pallas as pl
from jax.experimental.pallas import tpu as pltpu
from jax.sharding import PartitionSpec as P

BLOCK = 128
GATHER_LIMIT = 8 * 1024 * 1024


def block_hits(position, block_total):
    return (position[:, None] // BLOCK == jnp.arange(block_total, dtype=jnp.int32)[None, :]).astype(
        jnp.float32
    )


def reducing_body(curl_tiles, gradient, a_pattern, g_pattern):
    row_count = lax.axis_size("row")
    row_pos = lax.axis_index("row")
    col_pos = lax.axis_index("col")
    rows_here = curl_tiles.shape[1]
    span_rows = curl_tiles.shape[2]
    fine_blocks = a_pattern.shape[0]
    strided_total = row_count * rows_here
    offsets = jnp.arange(rows_here, dtype=jnp.int32)
    column_index = (
        jnp.arange(row_count, dtype=jnp.int32)[:, None] * span_rows
        + col_pos * rows_here
        + offsets[None, :]
    ).reshape(-1)
    row_index = row_pos * span_rows + jnp.arange(span_rows, dtype=jnp.int32)
    own_index = row_pos * span_rows + col_pos * rows_here + offsets
    picked = jnp.dot(block_hits(row_index, fine_blocks), a_pattern.astype(jnp.float32))
    keep_a = jnp.dot(block_hits(column_index, fine_blocks), picked.T)
    masked_a = curl_tiles.reshape(strided_total, span_rows) * keep_a.astype(jnp.bfloat16)
    keep_g = jnp.dot(block_hits(own_index, fine_blocks), g_pattern.astype(jnp.float32))
    masked_g = gradient * jnp.repeat(keep_g, BLOCK, axis=1).astype(jnp.bfloat16)
    g_group = lax.all_gather(masked_g, "col", axis=0, tiled=True)
    g_strided = lax.all_gather(masked_g, "row", axis=0, tiled=True)
    product_t = lax.psum_scatter(
        lax.dot_general(
            g_strided, masked_a, (((0,), (0,)), ((), ())), preferred_element_type=jnp.float32
        ),
        "col",
        scatter_dimension=0,
        tiled=True,
    )
    return lax.psum_scatter(
        lax.dot_general(
            g_group.astype(jnp.float32),
            product_t,
            (((0,), (1,)), ((), ())),
            precision=lax.Precision.HIGHEST,
            preferred_element_type=jnp.float32,
        ),
        "row",
        scatter_dimension=0,
        tiled=True,
    )


def ring_row(position, count):
    return jnp.where(position < count // 2, 2 * position, 2 * (count - 1 - position) + 1)


def ring_position(row, count):
    return jnp.where(row % 2 == 0, row // 2, count - 1 - row // 2)


def ring_rows(count):
    return list(range(0, count, 2)) + list(range(count - 1, 0, -2))


def layout(count, rows_here, coarse):
    a_rows = count * rows_here
    col_blocks = coarse // 4 // BLOCK
    row_blocks = -(-(coarse // count + 64) // BLOCK)
    crossing = a_rows + (2 * col_blocks + row_blocks) * rows_here
    share = a_rows + (col_blocks + row_blocks) * rows_here
    return a_rows, col_blocks, row_blocks, crossing, share


def first_window(row, count, coarse):
    return (row * (coarse // count)) // BLOCK


def aligned(start):
    return pl.multiple_of(start, 32)


def put(out_ref, at, ref, start, rows):
    out_ref[at : at + rows, :] = ref[pl.ds(start, rows), :]
    return at + rows


def cut_kernel(count, rows_here, coarse, items, *refs):
    a_rows, col_blocks, row_blocks, _, _ = layout(count, rows_here, coarse)
    row, col = lax.axis_index("row"), lax.axis_index("col")
    second = col % 2 == 1
    for (sources, steps, over), out_ref in zip(items, refs[len(refs) - len(items) :]):
        step = jnp.where(second, steps[1] + count, steps[0] + count)
        there = ring_row(lax.rem(ring_position(row, count) + step, count), count)
        half = aligned(a_rows + ((col // 2) ^ over) * (2 * col_blocks * rows_here))
        window = aligned(a_rows + first_window(there, count, coarse) * rows_here)
        at = 0
        for start, n in ((0, a_rows), (half, 2 * col_blocks * rows_here), (window, row_blocks * rows_here)):
            part = refs[sources[0]][pl.ds(start, n), :]
            if sources[1] != sources[0]:
                part = jnp.where(second, refs[sources[1]][pl.ds(start, n), :], part)
            out_ref[at : at + n, :] = part
            at += n


def pack_kernel(count, rows_here, coarse, a_pattern, g_pattern, a_ref, g_ref, out_ref):
    row = lax.axis_index("row")
    a_rows = layout(count, rows_here, coarse)[0]
    for k in range(count):
        out_ref[k * rows_here : (k + 1) * rows_here, :] = jnp.where(a_pattern[row, k] != 0, a_ref[k], 0)
    for j in range(coarse // BLOCK):
        out_ref[a_rows + j * rows_here : a_rows + (j + 1) * rows_here, :] = jnp.where(
            g_pattern[row, j] != 0, g_ref[:, j * BLOCK : (j + 1) * BLOCK], 0
        )


class Piece:
    def __init__(self, kind, ref, begin, sizes):
        self.kind, self.ref, self.begin, self.sizes = kind, ref, begin, sizes

    def tiles(self):
        return self.ref[self.begin : self.begin + self.sizes[0], :]

    def columns(self, rows_here, col):
        a_rows, col_blocks = self.sizes[:2]
        start = self.begin + a_rows
        if self.kind == "whole":
            start = aligned(start + col * (col_blocks * rows_here))
        elif self.kind == "cross":
            start = aligned(start + (col % 2) * (col_blocks * rows_here))
        return start

    def window(self, rows_here, first):
        a_rows, col_blocks = self.sizes[:2]
        start = self.begin + a_rows
        if self.kind == "whole":
            return aligned(start + first * rows_here)
        return start + (2 if self.kind == "cross" else 1) * col_blocks * rows_here


def pieces_of(spec, refs, sizes):
    return {key: Piece(kind, refs[index], begin, sizes) for key, (kind, index, begin) in spec.items()}


def collect_kernel(count, rows_here, coarse, spec, *refs):
    sizes = layout(count, rows_here, coarse)
    a_rows, col_blocks, row_blocks = sizes[:3]
    row, col = lax.axis_index("row"), lax.axis_index("col")
    first = first_window(row, count, coarse)
    for out_ref, owner in ((refs[-2], col), (refs[-1], col ^ 1)):
        at = 0
        for piece in pieces_of(spec, refs, sizes).values():
            at = put(out_ref, at, piece.ref, piece.begin, a_rows)
            at = put(out_ref, at, piece.ref, piece.columns(rows_here, owner), col_blocks * rows_here)
            at = put(out_ref, at, piece.ref, piece.window(rows_here, first), row_blocks * rows_here)


def place_kernel_part(pieces, count, rows_here, coarse, distances, g_cols, g_rows):
    _, col_blocks, row_blocks, _, _ = layout(count, rows_here, coarse)
    a_rows = count * rows_here
    row, col = lax.axis_index("row"), lax.axis_index("col")
    position = ring_position(row, count)
    first = first_window(row, count, coarse)
    for (d, m), piece in pieces.items():
        source = ring_row(lax.rem(position - d + count, count), count)
        if g_cols is not None:
            below = pl.ds(aligned(m * a_rows + source * rows_here), rows_here)
            start = piece.columns(rows_here, col)
            for j in range(col_blocks):
                g_cols[below, j * BLOCK : (j + 1) * BLOCK] = piece.ref[pl.ds(start + j * rows_here, rows_here), :]
        if d in distances:
            below = pl.ds(aligned(distances.index(d) * BLOCK + (col ^ m) * rows_here), rows_here)
            start = piece.window(rows_here, first)
            for j in range(row_blocks):
                g_rows[below, j * BLOCK : (j + 1) * BLOCK] = piece.ref[pl.ds(start + j * rows_here, rows_here), :]


def window_rows(row, count, coarse, g_rows, turned):
    out_rows = coarse // count
    turned[...] = jnp.transpose(g_rows[...])
    shift = pl.multiple_of(row * out_rows - first_window(row, count, coarse) * BLOCK, 64)
    return turned[pl.ds(shift, out_rows), :]


def partial_product(pieces, m, distances, g_turned):
    part = None
    for i in range(0, len(distances), 2):
        pair = distances[i : i + 2]
        tiles = [pieces[d, m].tiles() for d in pair]
        term = lax.dot_general(
            g_turned[:, i * BLOCK : (i + len(pair)) * BLOCK],
            tiles[0] if len(tiles) == 1 else jnp.concatenate(tiles, axis=1),
            (((1,), (1,)), ((), ())),
            preferred_element_type=jnp.float32,
        )
        part = term if part is None else part + term
    return part


def early_kernel(count, rows_here, coarse, spec, distances, *refs):
    part_ref, g_cols, g_rows, turned = refs[-4:]
    sizes = layout(count, rows_here, coarse)
    a_rows = sizes[0]
    pieces = pieces_of(spec, refs, sizes)
    place_kernel_part(pieces, count, rows_here, coarse, distances, g_cols, g_rows)
    g_turned = window_rows(lax.axis_index("row"), count, coarse, g_rows, turned)
    for m in range(4):
        part_ref[:, m * a_rows : (m + 1) * a_rows] = partial_product(pieces, m, distances, g_turned)


def product_kernel(count, rows_here, coarse, late, spec, distances, *refs):
    part_ref, g_early, out_ref, g_cols, g_rows, turned, terms = refs[-7:]
    out_rows = out_ref.shape[0]
    sizes = layout(count, rows_here, coarse)
    a_rows = sizes[0]
    pieces = pieces_of(spec, refs, sizes)
    g_cols[...] = g_early[...]
    place_kernel_part({key: pieces[key] for key in late}, count, rows_here, coarse, distances, g_cols, g_rows)
    rest = {key: piece for key, piece in pieces.items() if key not in late}
    place_kernel_part(rest, count, rows_here, coarse, distances, None, g_rows)
    g_turned = window_rows(lax.axis_index("row"), count, coarse, g_rows, turned)
    for m in range(4):
        columns = slice(m * a_rows, (m + 1) * a_rows)
        part = part_ref[:, columns] + partial_product(pieces, m, distances, g_turned)
        high = part.astype(jnp.bfloat16)
        terms[:out_rows, columns] = high
        terms[out_rows:, columns] = (part - high.astype(jnp.float32)).astype(jnp.bfloat16)
    total = jnp.dot(terms[...], g_cols[...], preferred_element_type=jnp.float32)
    out_ref[...] = total[:out_rows] + total[out_rows:]


def gathering_body(count, curl_tiles, gradient, a_pattern, g_pattern):
    rows_here = curl_tiles.shape[1]
    coarse = gradient.shape[1]
    out_rows, out_cols = coarse // count, coarse // 4
    a_rows, _, row_blocks, crossing, share = layout(count, rows_here, coarse)
    packed = a_rows + coarse // BLOCK * rows_here
    whole, scalars = pl.BlockSpec(memory_space=pltpu.VMEM), pl.BlockSpec(memory_space=pltpu.SMEM)
    limit = pltpu.CompilerParams(vmem_limit_bytes=8 * 1024 * 1024)
    sizes = (count, rows_here, coarse)
    axes = ("row", "col")

    def rows(n):
        return pltpu.VMEM((n, BLOCK), jnp.bfloat16)

    def turning(distances):
        shape = (distances * BLOCK, row_blocks * BLOCK)
        return [pltpu.VMEM(shape, jnp.bfloat16), pltpu.VMEM(shape[::-1], jnp.bfloat16)]

    def call(kernel, out, operands, name, *given, **options):
        return pl.pallas_call(
            functools.partial(kernel, *sizes, *given),
            out_shape=out,
            in_specs=options.pop("in_specs", [whole] * len(operands)),
            out_specs=[whole] * len(out) if isinstance(out, list) else whole,
            name=name,
            **options,
        )(*operands)

    order = ring_rows(count)

    def along(step):
        return [
            (order[p] * 4 + c, order[(p + step) % count] * 4 + c) for p in range(count) for c in range(4)
        ]

    def across(piece, mask):
        return lax.ppermute(piece, axes, [(i, i ^ mask) for i in range(4 * count)])

    forward, backward = along(1), along(-1)
    half = count // 2
    own = call(
        pack_kernel,
        rows(packed),
        (a_pattern, g_pattern, curl_tiles, gradient),
        "pack",
        in_specs=[scalars] * 2 + [whole] * 2,
    )
    held = {(0, 0): ("whole", own, 0), (0, 2): ("whole", across(own, 2), 0)}

    def operands_of(pieces):
        buffers, spec = [], {}
        for key, (kind, buffer, begin) in pieces.items():
            if not any(buffer is b for b in buffers):
                buffers.append(buffer)
            spec[key] = (kind, [buffer is b for b in buffers].index(True), begin)
        return buffers, spec

    def exchange(pieces, *over):
        buffers, spec = operands_of(pieces)
        mine, theirs = call(
            collect_kernel,
            [rows(len(pieces) * share)] * 2,
            [*buffers, *over],
            "collect",
            spec,
            compiler_params=limit,
        )
        theirs = across(theirs, 1)
        return {
            (d, m + other): ("share", (mine, theirs)[other], i * share)
            for i, (d, m) in enumerate(spec)
            for other in (0, 1)
        }

    def cut(items, *operands):
        return call(cut_kernel, [rows(crossing)] * len(items), operands, "cut", items, compiler_params=limit)

    chain = {m: (own, own) for m in (0, 2)}
    for step, m in ((step, m) for step in range(1, half) for m in (0, 2)):
        ahead, back = chain[m]
        kind = "whole"
        if m == 2 and step == half - 1:
            ahead, back = cut([((0, 0), (1, 1), 0), ((1, 1), (-1, -1), 0)], ahead, back)
            kind = "cross"
        ways = [[(i, j ^ m) if step == 1 else (i, j) for i, j in way] for way in (forward, backward)]
        back, ahead = lax.ppermute(back, axes, ways[1]), lax.ppermute(ahead, axes, ways[0])
        chain[m] = ahead, back
        held[step, m], held[count - step, m] = (kind, ahead, 0), (kind, back, 0)
    split = [pair for pair in forward if pair[0] % 2 == 1] + [pair for pair in backward if pair[0] % 2 == 0]
    straight, diagonal = cut(
        [((1, 0), (-1, 1), 0), ((1, 0), (-1, 1), 1)], held[half - 1, 0][1], held[half + 1, 0][1]
    )
    held[half, 2] = ("cross", lax.ppermute(diagonal, axes, [(i, j ^ 2) for i, j in split]), 0)
    held[half, 0] = ("cross", lax.ppermute(straight, axes, split), 0)
    early = {key: held[key] for key in held if min(key[0], count - key[0]) < half - key[1] // 2}
    early = dict(sorted(early.items()))
    got = exchange(early)
    distances = [d for d in range(count) if (d, 0) in early and (d, 2) in early]
    buffers, spec = operands_of(got)
    part, g_cols = call(
        early_kernel,
        [
            pltpu.VMEM((out_rows, 4 * a_rows), jnp.float32),
            pltpu.VMEM((4 * a_rows, out_cols), jnp.bfloat16),
        ],
        buffers,
        "early",
        spec,
        distances,
        scratch_shapes=turning(len(distances)),
        compiler_params=limit,
    )
    late = {key: piece for key, piece in reversed(held.items()) if key not in early}
    late.update({(d, m + 1): (kind, across(piece, 1), begin) for (d, m), (kind, piece, begin) in list(late.items())})
    late_distances = [d for d in range(count) if d not in distances]
    last_pieces = {**late, **{key: p for key, p in got.items() if key[0] in late_distances}}
    buffers, spec = operands_of(last_pieces)
    return call(
        product_kernel,
        jax.ShapeDtypeStruct((out_rows, out_cols), jnp.float32),
        buffers + [part, g_cols],
        "product",
        tuple(late),
        spec,
        late_distances,
        scratch_shapes=[
            pltpu.VMEM((4 * a_rows, out_cols), jnp.bfloat16),
            *turning(len(late_distances)),
            pltpu.VMEM((2 * out_rows, 4 * a_rows), jnp.bfloat16),
        ],
        compiler_params=limit,
    )


def gathers(mesh, curl_tiles, gradient):
    count, width = mesh.shape["row"], mesh.shape["col"]
    coarse = gradient.shape[1]
    return (
        width == 4
        and count % 2 == 0
        and count >= 8
        and curl_tiles.shape[2] // count == BLOCK
        and curl_tiles.shape[1] // width == 32
        and coarse % (width * BLOCK) == 0
        and coarse % (count * 64) == 0
        and 2 * (curl_tiles.size + gradient.size) <= GATHER_LIMIT
    )


def solution(mesh):
    placed = (P(None, "col", "row"), P(("row", "col"), None), P(), P())

    def run(curl_tiles, gradient, a_pattern, g_pattern):
        body = reducing_body
        if gathers(mesh, curl_tiles, gradient):
            body = functools.partial(gathering_body, mesh.shape["row"])
        return jax.shard_map(
            body, mesh=mesh, in_specs=placed, out_specs=P("row", "col"), check_vma=False
        )(curl_tiles, gradient, a_pattern, g_pattern)

    return run
```
